256 devices in a mesh: ctx: 32 (over x_hi, z, core), tp: 8 (over x_lo, y).
Axes of the slice: x: 4 (x_hi: 2, x_lo: 2; x = x_hi * 2 + x_lo), y: 4, z: 8, core: 2. Of those that a mesh axis runs over, the one named last changes fastest.
Arguments:
- hidden: bfloat16 [4096, 7168], P('ctx', 'tp'), may hold values from -500 to 500
- embed: bfloat16 [4096, 7168], P('ctx', 'tp'), may hold values from -500 to 500
- gain_hidden: float32 [7168], P('tp'), may hold values from 0.1 to 1.9
- gain_embed: float32 [7168], P('tp'), may hold values from 0.1 to 1.9
- proj_hidden: bfloat16 [7168, 576], P('tp'), may hold values from -0.0625 to 0.0625
- proj_embed: bfloat16 [7168, 576], P('tp'), may hold values from -0.0625 to 0.0625
- gain_latent: float32 [512], replicated, may hold values from 0.1 to 1.9
- key_up: bfloat16 [512, 8192], P(None, 'tp'), may hold values from -0.25 to 0.25
- value_up: bfloat16 [512, 8192], P(None, 'tp'), may hold values from -0.25 to 0.25
- queries: bfloat16 [4096, 12288], P('ctx', 'tp'), may hold values from -60 to 60
- grad_out: bfloat16 [4096, 8192], P('ctx', 'tp'), may hold values from -6 to 6
Outputs:
- attended: bfloat16 [4096, 8192], P('ctx', 'tp')
- grad_queries: bfloat16 [4096, 12288], P('ctx', 'tp')
- grad_hidden: bfloat16 [4096, 7168], P('ctx', 'tp')
- grad_embed: bfloat16 [4096, 7168], P('ctx', 'tp')
The draws below stay inside these ranges and needn't reach their ends.
All inputs are finite; a program needn't handle non-finite values.
Results may differ from the reference program's by a relative error of at most 0.019.
The reference program's roundings to bfloat16 on the way count: a program that leaves them out, or rounds other values in their place, can miss the bound.
Values may be sent and summed in bfloat16 or wider, within the bound.
No kernel may reach another device: no remote copies, remote signals or barrier semaphores. Data moves between devices by JAX's collectives and lax.ppermute only.
A program may use at most 128 MiB of HBM per device.

```python
import math
import jax
import jax.numpy as jnp
from jax import lax

D = 7168
LAT = 512
ROPE = 64
NOPE = 128
VDIM = 128
H = 64
SEQ = 4096
N_CTX = 32


def feature_values(key, row_count, column_count):
    splits = jax.random.split(key, 3)
    column_ramp = jnp.arange(column_count, dtype=jnp.float32) / column_count
    base_values = jnp.clip(jax.random.normal(splits[0], (row_count, column_count), jnp.float32), -6.0, 6.0)
    row_scale = jnp.exp(jax.random.uniform(splits[1], (row_count, 1), jnp.float32, 0.0, math.log(10.0)))
    column_scale = 3.0 ** column_ramp * jnp.exp(jax.random.uniform(splits[2], (column_count,), jnp.float32, 0.0, math.log(3.4)))
    return base_values * row_scale * column_scale / 3.0


def draw_hidden(key, part):
    return feature_values(jax.random.fold_in(key, 101), SEQ, D).astype(jnp.bfloat16)


def draw_embed(key, part):
    return feature_values(jax.random.fold_in(key, 202), SEQ, D).astype(jnp.bfloat16)


def draw_queries(key, part):
    splits = jax.random.split(jax.random.fold_in(key, 303), 1)
    array_shape = (SEQ, H * (NOPE + ROPE))
    values = 2.5 * jnp.clip(jax.random.normal(splits[0], array_shape, jnp.float32), -6.0, 6.0)
    return values.astype(jnp.bfloat16)


def shard_levels(own_key, extent, cuts, low, top_value):
    def one(axis_at, blocks):
        heights = jax.random.uniform(jax.random.fold_in(jax.random.fold_in(own_key, 6), axis_at), (blocks,), jnp.float32, low / len(cuts), top_value / len(cuts))
        return jnp.repeat(jnp.exp(heights), extent[axis_at] // blocks).reshape((-1,) + (1,) * (len(extent) - axis_at - 1))

    level = one(*cuts[0])
    for cut in cuts[1:]:
        level = level * one(*cut)
    return level


def centred(key, extent, spread, limit, cuts=(), kind=jnp.bfloat16):
    values = jax.random.normal(key, extent, jnp.float32) * spread
    if len(cuts) > 0:
        values = shard_levels(key, extent, cuts, -0.22, 0.18) * values
    return jnp.clip(values, min=-limit, max=limit).astype(kind)


def setup_inputs(seed: int = 0) -> dict:
    seeds = jax.random.split(jax.random.key(seed), 12)
    return {
        "hidden": draw_hidden(jax.random.fold_in(seeds[11], 71), 0),
        "embed": draw_embed(jax.random.fold_in(seeds[11], 71), 0),
        "gain_hidden": jnp.clip(1.0 + 0.18 * jax.random.normal(seeds[2], (D,), jnp.float32), 0.1, 1.9),
        "gain_embed": jnp.clip(1.0 + 0.18 * jax.random.normal(seeds[3], (D,), jnp.float32), 0.1, 1.9),
        "proj_hidden": centred(seeds[4], (D, LAT + ROPE), D ** -0.5, 0.0625, ((0, 8),)),
        "proj_embed": centred(seeds[5], (D, LAT + ROPE), D ** -0.5, 0.0625, ((0, 8),)),
        "gain_latent": jnp.clip(1.0 + 0.18 * jax.random.normal(seeds[6], (LAT,), jnp.float32), 0.1, 1.9),
        "key_up": centred(seeds[7], (LAT, H * NOPE), LAT ** -0.5, 0.25, ((1, 8),)),
        "value_up": centred(seeds[8], (LAT, H * VDIM), LAT ** -0.5, 0.25, ((1, 8),)),
        "queries": draw_queries(jax.random.fold_in(seeds[11], 71), 0),
        "grad_out": centred(seeds[10], (SEQ, H * VDIM), 1.0, 6.0, ((0, 32), (1, 8))),
    }


EPSILON = 1e-06
ROTARY_BASE = 10000.0

def rounded(values):
    return lax.optimization_barrier(values.astype(jnp.bfloat16)).astype(jnp.float32)

def rotation(positions):
    pair_count = ROPE // 2
    frequency = ROTARY_BASE ** (-jnp.arange(pair_count, dtype=jnp.float32) / pair_count)
    angles = positions.astype(jnp.float32)[:, None] * frequency[None, :]
    return (jnp.cos(angles), jnp.sin(angles))

def rotate_pairs(values, cos_table, sin_table):
    pair_count = ROPE // 2
    first_half = values[..., :pair_count]
    second_half = values[..., pair_count:]
    return jnp.concatenate([first_half * cos_table - second_half * sin_table, first_half * sin_table + second_half * cos_table], axis=-1)

def unrotate(values, cos_table, sin_table):
    pair_count = ROPE // 2
    first_half = values[..., :pair_count]
    second_half = values[..., pair_count:]
    return jnp.concatenate([first_half * cos_table + second_half * sin_table, second_half * cos_table - first_half * sin_table], axis=-1)

def to_positions(values):
    half_rows = values.shape[0] // (2 * N_CTX)
    trailing = values.shape[1:]
    shaped = values.reshape((N_CTX, 2, half_rows) + trailing)
    early_rows = shaped[:, 0].reshape((N_CTX * half_rows,) + trailing)
    late_rows = shaped[::-1, 1].reshape((N_CTX * half_rows,) + trailing)
    return jnp.concatenate([early_rows, late_rows], axis=0)

def to_rows(values):
    half_rows = values.shape[0] // (2 * N_CTX)
    trailing = values.shape[1:]
    early_rows = values[:N_CTX * half_rows].reshape((N_CTX, half_rows) + trailing)
    late_rows = values[N_CTX * half_rows:].reshape((N_CTX, half_rows) + trailing)[::-1]
    return jnp.stack([early_rows, late_rows], axis=1).reshape((2 * N_CTX * half_rows,) + trailing)

def reference(hidden, embed, gain_hidden, gain_embed, proj_hidden, proj_embed, gain_latent, key_up, value_up, queries, grad_out):
    seq_total = hidden.shape[0]
    head_count = key_up.shape[1] // NOPE
    score_scale = (NOPE + ROPE) ** (-0.5)
    key_block = max(256, seq_total // 16)
    hidden_pos = to_positions(hidden)
    embed_pos = to_positions(embed)
    next_embed = jnp.concatenate([embed_pos[1:], jnp.zeros((1, embed.shape[1]), embed.dtype)], axis=0)
    hidden_wide = hidden_pos.astype(jnp.float32)
    next_wide = next_embed.astype(jnp.float32)
    inv_hidden = lax.rsqrt(lax.optimization_barrier(jnp.sum(hidden_wide * hidden_wide, axis=1, keepdims=True)) / D + EPSILON)
    inv_next = lax.rsqrt(lax.optimization_barrier(jnp.sum(next_wide * next_wide, axis=1, keepdims=True)) / D + EPSILON)
    scaled_hidden = (hidden_wide * gain_hidden).astype(jnp.bfloat16)
    scaled_next = (next_wide * gain_embed).astype(jnp.bfloat16)
    part_hidden = jnp.dot(scaled_hidden, proj_hidden, preferred_element_type=jnp.float32)
    part_next = jnp.dot(scaled_next, proj_embed, preferred_element_type=jnp.float32)
    latent = inv_hidden * part_hidden + inv_next * part_next
    leading = latent[:, :LAT]
    inv_latent = lax.rsqrt(lax.optimization_barrier(jnp.mean(leading * leading, axis=1, keepdims=True)) + EPSILON)
    key_latent = (leading * inv_latent * gain_latent).astype(jnp.bfloat16)
    positions = jnp.arange(seq_total, dtype=jnp.int32)
    cos_table, sin_table = rotation(positions)
    key_rope = rotate_pairs(latent[:, LAT:], cos_table, sin_table).astype(jnp.bfloat16)
    key_table = jnp.concatenate([key_latent, key_rope], axis=1)
    query_heads = to_positions(queries).reshape(seq_total, head_count, NOPE + ROPE).astype(jnp.float32)
    query_rot = rotate_pairs(query_heads[..., NOPE:], cos_table[:, None], sin_table[:, None]).astype(jnp.bfloat16)
    key_up_heads = key_up.reshape(LAT, head_count, NOPE).astype(jnp.float32)
    value_up_heads = value_up.reshape(LAT, head_count, VDIM).astype(jnp.float32)
    query_latent = jnp.einsum('shn,lhn->shl', query_heads[..., :NOPE], key_up_heads).astype(jnp.bfloat16)
    query_full = jnp.swapaxes(jnp.concatenate([query_latent, query_rot], axis=2), 0, 1)
    grad_heads = to_positions(grad_out).reshape(seq_total, head_count, VDIM).astype(jnp.float32)
    grad_latent = jnp.swapaxes(jnp.einsum('shv,lhv->shl', grad_heads, value_up_heads).astype(jnp.bfloat16), 0, 1)
    grad_keys = jnp.zeros((seq_total, LAT + ROPE), jnp.float32)
    out_blocks = []
    grad_query_blocks = []
    for block_index in range(seq_total // key_block):
        first_row = block_index * key_block
        last_row = first_row + key_block
        key_slab = key_table[:last_row].astype(jnp.float32)
        allowed = jnp.arange(last_row, dtype=jnp.int32)[None, :] <= jnp.arange(first_row, last_row, dtype=jnp.int32)[:, None]

        def per_head(state_keys, inputs):
            query_block, grad_block = inputs
            query_wide = query_block.astype(jnp.float32)
            grad_wide = grad_block.astype(jnp.float32)
            scores = jnp.dot(query_wide, key_slab.T, preferred_element_type=jnp.float32) * score_scale
            scores = jnp.where(allowed, scores, -jnp.inf)
            weights = jnp.exp(scores - lax.optimization_barrier(jnp.max(scores, axis=1, keepdims=True)))
            prob_wide = rounded(weights / lax.optimization_barrier(jnp.sum(weights, axis=1, keepdims=True)))
            out_latent = jnp.dot(prob_wide, key_slab[:, :LAT], preferred_element_type=jnp.float32)
            delta_rows = lax.optimization_barrier(jnp.sum(grad_wide * out_latent, axis=1, keepdims=True))
            grad_prob = jnp.dot(grad_wide, key_slab[:, :LAT].T, preferred_element_type=jnp.float32)
            grad_score = rounded(prob_wide * (grad_prob - delta_rows) * score_scale)
            grad_query = jnp.dot(grad_score, key_slab, preferred_element_type=jnp.float32)
            grad_lead = jnp.dot(grad_score.T, query_wide[:, :LAT], preferred_element_type=jnp.float32) + jnp.dot(prob_wide.T, grad_wide, preferred_element_type=jnp.float32)
            grad_tail = jnp.dot(grad_score.T, query_wide[:, LAT:], preferred_element_type=jnp.float32)
            return (state_keys + jnp.concatenate([grad_lead, grad_tail], axis=1), (out_latent.astype(jnp.bfloat16), grad_query))
        block_keys, (out_heads, grad_heads_q) = lax.scan(per_head, jnp.zeros((last_row, LAT + ROPE), jnp.float32), (query_full[:, first_row:last_row], grad_latent[:, first_row:last_row]))
        grad_keys = grad_keys + jnp.pad(block_keys, ((0, seq_total - last_row), (0, 0)))
        out_blocks.append(out_heads)
        grad_query_blocks.append(grad_heads_q)
    out_all = jnp.concatenate(out_blocks, axis=1)
    grad_query_all = jnp.concatenate(grad_query_blocks, axis=1)
    attended = jnp.einsum('hsl,lhv->shv', out_all.astype(jnp.float32), value_up_heads).astype(jnp.bfloat16).reshape(seq_total, head_count * VDIM)
    grad_lead_q = rounded(grad_query_all[..., :LAT])
    grad_nope = jnp.einsum('hsl,lhn->shn', grad_lead_q, key_up_heads)
    grad_rope = unrotate(jnp.swapaxes(grad_query_all[..., LAT:], 0, 1), cos_table[:, None], sin_table[:, None])
    grad_queries = jnp.concatenate([grad_nope, grad_rope], axis=2).astype(jnp.bfloat16).reshape(seq_total, head_count * (NOPE + ROPE))
    grad_rope_key = unrotate(grad_keys[:, LAT:], cos_table, sin_table)
    gained = gain_latent * grad_keys[:, :LAT]
    grad_leading = inv_latent * gained - inv_latent ** 3 * leading * lax.optimization_barrier(jnp.sum(gained * leading, axis=1, keepdims=True)) / LAT
    grad_lat = jnp.concatenate([grad_leading, grad_rope_key], axis=1)
    part_grad_hidden = (inv_hidden * grad_lat).astype(jnp.bfloat16)
    part_grad_next = (inv_next * grad_lat).astype(jnp.bfloat16)
    coef_hidden = lax.optimization_barrier(jnp.sum(grad_lat * part_hidden, axis=1, keepdims=True)) * inv_hidden ** 3 / D
    coef_next = lax.optimization_barrier(jnp.sum(grad_lat * part_next, axis=1, keepdims=True)) * inv_next ** 3 / D
    grad_hidden = (gain_hidden * jnp.dot(part_grad_hidden, proj_hidden.T, preferred_element_type=jnp.float32) - coef_hidden * hidden_wide).astype(jnp.bfloat16)
    grad_next = gain_embed * jnp.dot(part_grad_next, proj_embed.T, preferred_element_type=jnp.float32) - coef_next * next_wide
    grad_embed = jnp.concatenate([jnp.zeros((1, grad_next.shape[1]), jnp.float32), grad_next[:-1]], axis=0).astype(jnp.bfloat16)
    return (to_rows(attended), to_rows(grad_queries), to_rows(grad_hidden), to_rows(grad_embed))
```

```python
import functools

import jax
import jax.numpy as jnp
from jax import lax
from jax.experimental import pallas as pl
from jax.experimental.pallas import tpu as pltpu
from jax.sharding import Mesh, PartitionSpec as P

D = 7168
LAT = 512
ROPE = 64
NOPE = 128
VDIM = 128
KEYW = LAT + ROPE
WIDE = 640

EPSILON = 1e-06
ROTARY_BASE = 10000.0
SCALE = (NOPE + ROPE) ** (-0.5)

CTX = ("xh", "z", "co")
TP = ("xl", "y")
XZ = ("xh", "z")
N_CTX = 32
N_TP = 8
HEADS = 8
HALF = 64
ROWS = 128
PIECE = ROWS // N_TP
SEG = HALF * HEADS
BLOCK = 512
STEPS = 9

bf16 = jnp.bfloat16
f32 = jnp.float32


def rotation(positions):
    pair_count = ROPE // 2
    frequency = ROTARY_BASE ** (-jnp.arange(pair_count, dtype=f32) / pair_count)
    angles = positions.astype(f32)[:, None] * frequency[None, :]
    return (jnp.cos(angles), jnp.sin(angles))


def rotate_pairs(values, cos_table, sin_table):
    a, b = jnp.split(values, 2, axis=-1)
    return jnp.concatenate(
        [a * cos_table - b * sin_table, a * sin_table + b * cos_table], axis=-1
    )


def unrotate(values, cos_table, sin_table):
    a, b = jnp.split(values, 2, axis=-1)
    return jnp.concatenate(
        [a * cos_table + b * sin_table, b * cos_table - a * sin_table], axis=-1
    )


def row_positions(ctx, rows):
    return jnp.where(rows < HALF, ctx * HALF + rows, (63 - ctx) * HALF + rows - HALF)


def gather_copies(x, axes, n):
    copies = jnp.broadcast_to(x[None], (n, *x.shape))
    return lax.all_to_all(copies, axes, split_axis=0, concat_axis=0, tiled=True)


def edge_exchange(first_row, second_row):
    down = [(i + 1, i) for i in range(N_CTX - 1)]
    up = [(i, i + 1) for i in range(N_CTX - 1)]
    return lax.ppermute(first_row, CTX, down), lax.ppermute(second_row, CTX, up)


def attention_kernel(
    where_ref,
    mine_ref,
    other_ref,
    q_ref,
    qt_ref,
    g_ref,
    gt_ref,
    o_ref,
    lead_ref,
    tail_ref,
    dmine_ref,
    dother_ref,
    keys,
    s_buf,
    dp_buf,
    m_buf,
    l_buf,
    a_buf,
    ot_buf,
    dqt_buf,
    dk_buf,
    sems,
):
    ctx = where_ref[0]
    core = where_ref[1]
    copies = [
        pltpu.make_async_copy(mine_ref, keys.at[core], sems.at[0]),
        pltpu.make_async_copy(other_ref, keys.at[1 - core], sems.at[1]),
    ]
    for copy in copies:
        copy.start()
    m_buf[...] = jnp.full_like(m_buf, -jnp.inf)
    l_buf[...] = jnp.zeros_like(l_buf)
    a_buf[...] = jnp.zeros_like(a_buf)
    ot_buf[...] = jnp.zeros_like(ot_buf)
    dqt_buf[...] = jnp.zeros_like(dqt_buf)
    dk_buf[...] = jnp.zeros_like(dk_buf)
    for copy in copies:
        copy.wait()

    group = ctx // 8
    early_steps = group + 1

    def locate(i):
        late = i >= early_steps
        j = i - early_steps
        half = jnp.logical_and(late, j >= 4).astype(jnp.int32)
        block = jnp.where(late, jnp.where(j >= 4, group + j - 4, j), i)
        return late.astype(jnp.int32), half, block

    def slab(half, block):
        xh = block // 2
        at = pl.multiple_of((block % 2) * 64, 64)
        return jnp.concatenate(
            [
                keys[co, half * 4 + y, xh, pl.ds(at, 64), :]
                for co in range(2)
                for y in range(4)
            ],
            axis=0,
        )

    def nn(a, b):
        return jnp.dot(a, b, preferred_element_type=f32)

    def first(i, carry):
        seg, half, block = locate(i)
        k = slab(half, block)
        s = nn(k, qt_ref[seg]) * SCALE
        idx = lax.broadcasted_iota(jnp.int32, (BLOCK, 1), 0)
        owner = block * 8 + ((idx // 16) % 4) * 2 + idx // 256
        within = ((idx // 64) % 4) * 16 + idx % 16
        key_pos = jnp.where(half == 0, owner, 63 - owner) * 64 + within
        row = lax.broadcasted_iota(jnp.int32, (1, SEG), 1)
        q_pos = jnp.where(seg == 0, ctx, 63 - ctx) * 64 + row % 64
        s = jnp.where(key_pos <= q_pos, s, -jnp.inf)
        s_buf[i] = s
        dp = nn(k[:, :LAT], gt_ref[seg])
        dp_buf[i] = dp
        m_old = m_buf[seg]
        m_new = jnp.maximum(m_old, jnp.max(s, axis=0, keepdims=True))
        alpha = jnp.exp(m_old - m_new)
        e = jnp.exp(s - m_new)
        m_buf[seg] = m_new
        l_buf[seg] = l_buf[seg] * alpha + jnp.sum(e, axis=0, keepdims=True)
        a_buf[seg] = a_buf[seg] * alpha + jnp.sum(e * dp, axis=0, keepdims=True)
        return carry

    lax.fori_loop(0, STEPS, first, 0)

    def second(i, carry):
        seg, half, block = locate(i)
        k = slab(half, block)
        inv = 1.0 / l_buf[seg]
        delta = a_buf[seg] * inv
        p = (jnp.exp(s_buf[i] - m_buf[seg]) * inv).astype(bf16)
        ds = (p.astype(f32) * (dp_buf[i] - delta) * SCALE).astype(bf16)
        kt = k.T
        ot_buf[seg] += nn(kt[:LAT], p)
        dqt_buf[seg] += nn(kt, ds)
        lead = nn(ds, q_ref[seg, :, :LAT]) + nn(p, g_ref[seg])
        tail = nn(ds, q_ref[seg, :, LAT:])
        xh = block // 2
        at = pl.multiple_of((block % 2) * 64, 64)
        for co in range(2):
            for y in range(4):
                j = (co * 4 + y) * 64
                dk_buf[co, half * 4 + y, xh, pl.ds(at, 64), :LAT] += lead[j : j + 64]
                dk_buf[co, half * 4 + y, xh, pl.ds(at, 64), LAT:] += tail[j : j + 64]
        return carry

    lax.fori_loop(0, STEPS, second, 0)

    for seg in range(2):
        o_ref[seg] = ot_buf[seg].astype(bf16).T
        lead_ref[seg] = dqt_buf[seg, :LAT].astype(bf16).T
        tail_ref[seg] = dqt_buf[seg, LAT:].T

    def put(t, carry):
        dmine_ref[t] = dk_buf[core, t].astype(bf16)
        dother_ref[t] = dk_buf[1 - core, t].astype(bf16)
        return carry

    lax.fori_loop(0, N_TP, put, 0)


def attention(where, mine, other, q, qt, g, gt):
    vmem = pl.BlockSpec(memory_space=pltpu.VMEM)
    hbm = pl.BlockSpec(memory_space=pl.ANY)
    half_keys = (N_TP, 2, 128, KEYW)
    return pl.pallas_call(
        attention_kernel,
        in_specs=[pl.BlockSpec(memory_space=pltpu.SMEM), hbm, hbm, vmem, vmem, vmem, vmem],
        out_specs=[vmem] * 5,
        out_shape=[
            jax.ShapeDtypeStruct((2, SEG, LAT), bf16),
            jax.ShapeDtypeStruct((2, SEG, LAT), bf16),
            jax.ShapeDtypeStruct((2, SEG, ROPE), f32),
            jax.ShapeDtypeStruct(half_keys, bf16),
            jax.ShapeDtypeStruct(half_keys, bf16),
        ],
        scratch_shapes=[
            pltpu.VMEM((2,) + half_keys, bf16),
            pltpu.VMEM((STEPS, BLOCK, SEG), f32),
            pltpu.VMEM((STEPS, BLOCK, SEG), f32),
            pltpu.VMEM((2, 1, SEG), f32),
            pltpu.VMEM((2, 1, SEG), f32),
            pltpu.VMEM((2, 1, SEG), f32),
            pltpu.VMEM((2, LAT, SEG), f32),
            pltpu.VMEM((2, KEYW, SEG), f32),
            pltpu.VMEM((2,) + half_keys, f32),
            pltpu.SemaphoreType.DMA((2,)),
        ],
        compiler_params=pltpu.CompilerParams(vmem_limit_bytes=62 * 1024 * 1024),
        cost_estimate=pl.CostEstimate(
            flops=14_000_000_000, bytes_accessed=20_000_000, transcendentals=4_000_000
        ),
        name="attention",
    )(where, mine, other, q, qt, g, gt)


def on_device(
    hidden,
    embed,
    gain_hidden,
    gain_embed,
    proj_hidden,
    proj_embed,
    gain_latent,
    key_up,
    value_up,
    queries,
    grad_out,
):
    ctx = lax.axis_index(CTX)
    core = lax.axis_index("co")
    tp = lax.axis_index(TP)
    last = ctx == N_CTX - 1

    after, before = edge_exchange(embed[0:1], embed[HALF : HALF + 1])
    after_early = jnp.where(last, embed[HALF : HALF + 1], after)
    next_embed = jnp.concatenate(
        [embed[1:HALF], after_early, embed[HALF + 1 :], before], axis=0
    )
    hidden_wide = hidden.astype(f32)
    next_wide = next_embed.astype(f32)
    part_hidden = jnp.dot(
        (hidden_wide * gain_hidden).astype(bf16), proj_hidden, preferred_element_type=f32
    )
    part_next = jnp.dot(
        (next_wide * gain_embed).astype(bf16), proj_embed, preferred_element_type=f32
    )
    spread = (ROWS, WIDE - KEYW)
    parts = jnp.concatenate(
        [
            part_hidden,
            jnp.broadcast_to(jnp.sum(hidden_wide * hidden_wide, axis=1, keepdims=True), spread),
            part_next,
            jnp.broadcast_to(jnp.sum(next_wide * next_wide, axis=1, keepdims=True), spread),
        ],
        axis=1,
    ).reshape(N_TP, PIECE, 2 * WIDE)
    parts = jnp.sum(lax.all_to_all(parts, TP, split_axis=0, concat_axis=0, tiled=True), axis=0)

    part_hidden, part_next = parts[:, :KEYW], parts[:, WIDE : WIDE + KEYW]
    inv_hidden = lax.rsqrt(parts[:, KEYW : KEYW + 1] / D + EPSILON)
    inv_next = lax.rsqrt(parts[:, WIDE + KEYW : WIDE + KEYW + 1] / D + EPSILON)
    latent = inv_hidden * part_hidden + inv_next * part_next
    leading = latent[:, :LAT]
    inv_latent = lax.rsqrt(jnp.mean(leading * leading, axis=1, keepdims=True) + EPSILON)
    piece_cos, piece_sin = rotation(row_positions(ctx, tp * PIECE + jnp.arange(PIECE)))
    key_piece = jnp.concatenate(
        [
            (leading * inv_latent * gain_latent).astype(bf16),
            rotate_pairs(latent[:, LAT:], piece_cos, piece_sin).astype(bf16),
        ],
        axis=1,
    )
    same = gather_copies(key_piece, XZ, 16).reshape(2, 128, KEYW)
    mine = gather_copies(same, TP, N_TP).reshape(N_TP, 2, 128, KEYW)
    other = lax.ppermute(mine, "co", [(0, 1), (1, 0)])

    cos_table, sin_table = rotation(row_positions(ctx, jnp.arange(ROWS)))
    cos_table = cos_table.reshape(2, 1, HALF, ROPE // 2)
    sin_table = sin_table.reshape(2, 1, HALF, ROPE // 2)
    key_up_heads = key_up.reshape(LAT, HEADS, NOPE)
    value_up_heads = value_up.reshape(LAT, HEADS, VDIM)
    query_heads = queries.reshape(2, HALF, HEADS, NOPE + ROPE).transpose(0, 2, 1, 3)
    query_rot = rotate_pairs(query_heads[..., NOPE:].astype(f32), cos_table, sin_table)
    query_latent = jnp.einsum(
        "ghsn,lhn->ghsl", query_heads[..., :NOPE], key_up_heads, preferred_element_type=f32
    )
    q = jnp.concatenate([query_latent.astype(bf16), query_rot.astype(bf16)], axis=3)
    q = q.reshape(2, SEG, KEYW)
    g = jnp.einsum(
        "gshv,lhv->ghsl",
        grad_out.reshape(2, HALF, HEADS, VDIM),
        value_up_heads,
        preferred_element_type=f32,
    )
    g = g.astype(bf16).reshape(2, SEG, LAT)
    where = jnp.stack([ctx, core]).astype(jnp.int32)
    o, lead, tail, dmine, dother = attention(
        where, mine, other, q, q.swapaxes(1, 2), g, g.swapaxes(1, 2)
    )

    received = lax.ppermute(dother, "co", [(0, 1), (1, 0)])
    dkey = (dmine.astype(f32) + received.astype(f32)).astype(bf16)
    dkey = lax.all_to_all(dkey, TP, split_axis=0, concat_axis=0, tiled=True)
    dkey = jnp.sum(dkey.astype(f32), axis=0).astype(bf16).reshape(16, PIECE, KEYW)
    dkey = lax.all_to_all(dkey, XZ, split_axis=0, concat_axis=0, tiled=True)
    dkey = jnp.sum(dkey.astype(f32), axis=0)

    attended = jnp.einsum(
        "ghsl,lhv->gshv",
        o.reshape(2, HEADS, HALF, LAT),
        value_up_heads,
        preferred_element_type=f32,
    )
    attended = attended.astype(bf16).reshape(ROWS, HEADS * VDIM)
    grad_nope = jnp.einsum(
        "ghsl,lhn->ghsn",
        lead.reshape(2, HEADS, HALF, LAT),
        key_up_heads,
        preferred_element_type=f32,
    )
    grad_rope = unrotate(tail.reshape(2, HEADS, HALF, ROPE), cos_table, sin_table)
    grad_queries = jnp.concatenate([grad_nope, grad_rope], axis=3).astype(bf16)
    grad_queries = grad_queries.transpose(0, 2, 1, 3).reshape(ROWS, HEADS * (NOPE + ROPE))

    gained = gain_latent * dkey[:, :LAT]
    dlatent = jnp.concatenate(
        [
            inv_latent * gained
            - inv_latent**3 * leading * jnp.sum(gained * leading, axis=1, keepdims=True) / LAT,
            unrotate(dkey[:, LAT:], piece_cos, piece_sin),
        ],
        axis=1,
    )
    coef_hidden = jnp.sum(dlatent * part_hidden, axis=1, keepdims=True) * inv_hidden**3 / D
    coef_next = jnp.sum(dlatent * part_next, axis=1, keepdims=True) * inv_next**3 / D

    def in_two(c):
        high = c.astype(bf16)
        low = (c - high.astype(f32)).astype(bf16)
        width = (PIECE, (WIDE - KEYW) // 2)
        return [jnp.broadcast_to(high, width), jnp.broadcast_to(low, width)]

    packed = jnp.concatenate(
        [(inv_hidden * dlatent).astype(bf16)]
        + in_two(coef_hidden)
        + [(inv_next * dlatent).astype(bf16)]
        + in_two(coef_next),
        axis=1,
    )
    packed = gather_copies(packed, TP, N_TP).reshape(ROWS, 2 * WIDE)

    def whole(block):
        high = block[:, KEYW : KEYW + 1].astype(f32)
        return block[:, :KEYW], high + block[:, WIDE - 1 :].astype(f32)

    dpart_hidden, coef_hidden = whole(packed[:, :WIDE])
    grad_hidden = (
        gain_hidden
        * jnp.einsum("rc,dc->rd", dpart_hidden, proj_hidden, preferred_element_type=f32)
        - coef_hidden * hidden_wide
    ).astype(bf16)

    nexts = packed[:, WIDE:]
    after, before = edge_exchange(nexts[ROWS - 1 :], nexts[HALF - 1 : HALF])
    before_late = jnp.where(last, nexts[HALF - 1 : HALF], after)
    shifted = jnp.concatenate(
        [before, nexts[: HALF - 1], before_late, nexts[HALF : ROWS - 1]], axis=0
    )
    dpart_next, coef_next = whole(shifted)
    grad_embed = (
        gain_embed
        * jnp.einsum("rc,dc->rd", dpart_next, proj_embed, preferred_element_type=f32)
        - coef_next * embed.astype(f32)
    ).astype(bf16)
    return (attended, grad_queries, grad_hidden, grad_embed)


def solution(mesh):
    axes = ("xh", "z", "co", "xl", "y")
    fine = Mesh(mesh.devices.reshape(2, 8, 2, 2, 4), axes)
    both = P(CTX, TP)
    placed = (
        both,
        both,
        P(TP),
        P(TP),
        P(TP, None),
        P(TP, None),
        P(),
        P(None, TP),
        P(None, TP),
        both,
        both,
    )
    return jax.shard_map(
        on_device,
        mesh=fine,
        in_specs=placed,
        out_specs=(both, both, both, both),
        check_vma=False,
    )
```

```python
import functools

import jax
import jax.numpy as jnp
from jax import lax
from jax.experimental import pallas as pl
from jax.experimental.pallas import tpu as pltpu
from jax.sharding import Mesh, PartitionSpec as P

D = 7168
LAT = 512
ROPE = 64
NOPE = 128
VDIM = 128
KEYW = LAT + ROPE
WIDE = 640

EPSILON = 1e-06
ROTARY_BASE = 10000.0
SCALE = (NOPE + ROPE) ** (-0.5)

CTX = ("xh", "z", "co")
TP = ("xl", "y")
XZ = ("xh", "z")
N_CTX = 32
N_TP = 8
HEADS = 8
HALF = 64
ROWS = 128
PIECE = ROWS // N_TP
SEG = HALF * HEADS
BLOCK = 512
STEPS = 9

bf16 = jnp.bfloat16
f32 = jnp.float32


def rotation(positions):
    pair_count = ROPE // 2
    frequency = ROTARY_BASE ** (-jnp.arange(pair_count, dtype=f32) / pair_count)
    angles = positions.astype(f32)[:, None] * frequency[None, :]
    return (jnp.cos(angles), jnp.sin(angles))


def rotate_pairs(values, cos_table, sin_table):
    a, b = jnp.split(values, 2, axis=-1)
    return jnp.concatenate(
        [a * cos_table - b * sin_table, a * sin_table + b * cos_table], axis=-1
    )


def unrotate(values, cos_table, sin_table):
    a, b = jnp.split(values, 2, axis=-1)
    return jnp.concatenate(
        [a * cos_table + b * sin_table, b * cos_table - a * sin_table], axis=-1
    )


def row_positions(ctx, rows):
    return jnp.where(rows < HALF, ctx * HALF + rows, (63 - ctx) * HALF + rows - HALF)


def gather_copies(x, axes, n):
    copies = jnp.broadcast_to(x[None], (n, *x.shape))
    return lax.all_to_all(copies, axes, split_axis=0, concat_axis=0, tiled=True)


def edge_exchange(first_row, second_row):
    down = [(i + 1, i) for i in range(N_CTX - 1)]
    up = [(i, i + 1) for i in range(N_CTX - 1)]
    return lax.ppermute(first_row, CTX, down), lax.ppermute(second_row, CTX, up)


def pack_keys(rows):
    lead = rows[..., :LAT].reshape(2, 128, 4, 128).transpose(0, 2, 1, 3).reshape(8, 128, 128)
    rope = jnp.concatenate([rows[0, :, LAT:KEYW], rows[1, :, LAT:KEYW]], axis=1)
    return jnp.concatenate([lead, rope[None]], axis=0)


def unpack_keys(tiles):
    lead = tiles[:8].reshape(2, 4, 128, 128).transpose(0, 2, 1, 3).reshape(2, 128, LAT)
    rope = jnp.stack([tiles[8, :, :ROPE], tiles[8, :, ROPE:]], axis=0)
    return jnp.concatenate([lead, rope, jnp.zeros_like(rope)], axis=2)


def attention_kernel(
    where_ref,
    mine_ref,
    other_ref,
    q_hbm,
    qt_hbm,
    g_hbm,
    gt_hbm,
    ot_hbm,
    leadt_hbm,
    tailt_hbm,
    dmine_ref,
    dother_ref,
    keys,
    q_ref,
    qt_ref,
    g_ref,
    gt_ref,
    s_buf,
    dp_buf,
    m_buf,
    l_buf,
    a_buf,
    ot_buf,
    dqt_buf,
    ot_out,
    lead_out,
    dk_buf,
    dk_out,
    sems,
    out_sems,
):
    ctx = where_ref[0]
    core = where_ref[1]
    copies = [
        pltpu.make_async_copy(source, target, sems.at[n])
        for n, (source, target) in enumerate(
            [
                (mine_ref, keys.at[core]),
                (qt_hbm, qt_ref),
                (gt_hbm, gt_ref),
                (other_ref, keys.at[1 - core]),
                (q_hbm, q_ref),
                (g_hbm, g_ref),
            ]
        )
    ]
    for copy in copies:
        copy.start()
    m_buf[...] = jnp.full_like(m_buf, -jnp.inf)
    l_buf[...] = jnp.zeros_like(l_buf)
    a_buf[...] = jnp.zeros_like(a_buf)
    ot_buf[...] = jnp.zeros_like(ot_buf)
    dqt_buf[...] = jnp.zeros_like(dqt_buf)

    def clear(t, carry):
        dk_buf[0, t] = jnp.zeros((9, 128, 128), f32)
        dk_buf[1, t] = jnp.zeros((9, 128, 128), f32)
        return carry

    lax.fori_loop(0, N_TP, clear, 0)
    for copy in copies[:4]:
        copy.wait()

    group = ctx // 8
    early_steps = group + 1

    def locate(i):
        late = i >= early_steps
        j = i - early_steps
        half = jnp.logical_and(late, j >= 4).astype(jnp.int32)
        block = jnp.where(late, jnp.where(j >= 4, group + j - 4, j), i)
        return late.astype(jnp.int32), half, block

    def slab(half, block):
        xh = block // 2
        at = pl.multiple_of((block % 2) * 64, 64)

        def tile(part):
            return jnp.concatenate(
                [
                    keys[co, half * 4 + y, part, pl.ds(at, 64), :]
                    for co in range(2)
                    for y in range(4)
                ],
                axis=0,
            )

        rope = tile(8)
        rope = jnp.where(xh == 0, rope[:, :ROPE], rope[:, ROPE:])
        return jnp.concatenate([tile(xh * 4 + c) for c in range(4)] + [rope], axis=1)

    def nn(a, b):
        return jnp.dot(a, b, preferred_element_type=f32)

    def first(i, carry):
        seg, half, block = locate(i)
        k = slab(half, block)
        s = nn(k, qt_ref[seg]) * SCALE
        idx = lax.broadcasted_iota(jnp.int32, (BLOCK, 1), 0)
        owner = block * 8 + ((idx // 16) % 4) * 2 + idx // 256
        within = ((idx // 64) % 4) * 16 + idx % 16
        key_pos = jnp.where(half == 0, owner, 63 - owner) * 64 + within
        row = lax.broadcasted_iota(jnp.int32, (1, SEG), 1)
        q_pos = jnp.where(seg == 0, ctx, 63 - ctx) * 64 + row % 64
        s = jnp.where(key_pos <= q_pos, s, -jnp.inf)
        s_buf[i] = s
        dp = nn(k[:, :LAT], gt_ref[seg])
        dp_buf[i] = dp
        m_old = m_buf[seg]
        m_new = jnp.maximum(m_old, jnp.max(s, axis=0, keepdims=True))
        alpha = jnp.exp(m_old - m_new)
        e = jnp.exp(s - m_new)
        m_buf[seg] = m_new
        l_buf[seg] = l_buf[seg] * alpha + jnp.sum(e, axis=0, keepdims=True)
        a_buf[seg] = a_buf[seg] * alpha + jnp.sum(e * dp, axis=0, keepdims=True)
        return carry

    lax.fori_loop(0, STEPS, first, 0)
    for copy in copies[4:]:
        copy.wait()

    def second(i, carry):
        seg, half, block = locate(i)
        k = slab(half, block)
        inv = 1.0 / l_buf[seg]
        delta = a_buf[seg] * inv
        p = (jnp.exp(s_buf[i] - m_buf[seg]) * inv).astype(bf16)
        ds = (p.astype(f32) * (dp_buf[i] - delta) * SCALE).astype(bf16)
        kt = k.T
        ot_buf[seg] += nn(kt[:LAT], p)
        dqt_buf[seg] += nn(kt, ds)
        lead = nn(ds, q_ref[seg, :, :LAT]) + nn(p, g_ref[seg])
        tail = nn(ds, q_ref[seg, :, LAT:])
        xh = block // 2
        at = pl.multiple_of((block % 2) * 64, 64)
        lane = lax.broadcasted_iota(jnp.int32, (1, 128), 1)
        tail = jnp.where(lane // ROPE == xh, jnp.concatenate([tail, tail], axis=1), 0.0)
        for co in range(2):
            for y in range(4):
                j = (co * 4 + y) * 64
                own = half * 4 + y
                for c in range(4):
                    dk_buf[co, own, xh * 4 + c, pl.ds(at, 64), :] += lead[
                        j : j + 64, c * 128 : c * 128 + 128
                    ]
                dk_buf[co, own, 8, pl.ds(at, 64), :] += tail[j : j + 64]
        return carry

    lax.fori_loop(0, STEPS, second, 0)

    sends = []

    def send(source, target):
        copy = pltpu.make_async_copy(source, target, out_sems.at[len(sends)])
        copy.start()
        sends.append(copy)

    send(dqt_buf.at[:, pl.ds(LAT, ROPE)], tailt_hbm)
    for t in range(N_TP):
        dk_out[0, t] = dk_buf[1 - core, t].astype(bf16)
        send(dk_out.at[0, t], dother_ref.at[t])
    for t in range(N_TP):
        dk_out[1, t] = dk_buf[core, t].astype(bf16)
        send(dk_out.at[1, t], dmine_ref.at[t])
    for seg in range(2):
        ot_out[seg] = ot_buf[seg].astype(bf16)
        send(ot_out.at[seg], ot_hbm.at[seg])
        lead_out[seg] = dqt_buf[seg, :LAT].astype(bf16)
        send(lead_out.at[seg], leadt_hbm.at[seg])
    for copy in sends:
        copy.wait()


def attention(where, mine, other, q, qt, g, gt):
    hbm = pl.BlockSpec(memory_space=pl.ANY)
    half_keys = (N_TP, 9, 128, 128)
    return pl.pallas_call(
        attention_kernel,
        in_specs=[pl.BlockSpec(memory_space=pltpu.SMEM)] + [hbm] * 6,
        out_specs=[hbm] * 5,
        out_shape=[
            jax.ShapeDtypeStruct((2, LAT, SEG), bf16),
            jax.ShapeDtypeStruct((2, LAT, SEG), bf16),
            jax.ShapeDtypeStruct((2, ROPE, SEG), f32),
            jax.ShapeDtypeStruct(half_keys, bf16),
            jax.ShapeDtypeStruct(half_keys, bf16),
        ],
        scratch_shapes=[
            pltpu.VMEM((2,) + half_keys, bf16),
            pltpu.VMEM((2, SEG, KEYW), bf16),
            pltpu.VMEM((2, KEYW, SEG), bf16),
            pltpu.VMEM((2, SEG, LAT), bf16),
            pltpu.VMEM((2, LAT, SEG), bf16),
            pltpu.VMEM((STEPS, BLOCK, SEG), f32),
            pltpu.VMEM((STEPS, BLOCK, SEG), f32),
            pltpu.VMEM((2, 1, SEG), f32),
            pltpu.VMEM((2, 1, SEG), f32),
            pltpu.VMEM((2, 1, SEG), f32),
            pltpu.VMEM((2, LAT, SEG), f32),
            pltpu.VMEM((2, KEYW, SEG), f32),
            pltpu.VMEM((2, LAT, SEG), bf16),
            pltpu.VMEM((2, LAT, SEG), bf16),
            pltpu.VMEM((2,) + half_keys, f32),
            pltpu.VMEM((2,) + half_keys, bf16),
            pltpu.SemaphoreType.DMA((6,)),
            pltpu.SemaphoreType.DMA((21,)),
        ],
        compiler_params=pltpu.CompilerParams(vmem_limit_bytes=58 * 1024 * 1024),
        cost_estimate=pl.CostEstimate(
            flops=14_000_000_000, bytes_accessed=20_000_000, transcendentals=4_000_000
        ),
        name="attention",
    )(where, mine, other, q, qt, g, gt)


def on_device(
    hidden,
    embed,
    gain_hidden,
    gain_embed,
    proj_hidden,
    proj_embed,
    gain_latent,
    key_up,
    value_up,
    queries,
    grad_out,
):
    ctx = lax.axis_index(CTX)
    core = lax.axis_index("co")
    tp = lax.axis_index(TP)
    last = ctx == N_CTX - 1

    after, before = edge_exchange(embed[0:1], embed[HALF : HALF + 1])
    after_early = jnp.where(last, embed[HALF : HALF + 1], after)
    next_embed = jnp.concatenate(
        [embed[1:HALF], after_early, embed[HALF + 1 :], before], axis=0
    )
    hidden_wide = hidden.astype(f32)
    next_wide = next_embed.astype(f32)
    part_hidden = jnp.dot(
        (hidden_wide * gain_hidden).astype(bf16), proj_hidden, preferred_element_type=f32
    )
    part_next = jnp.dot(
        (next_wide * gain_embed).astype(bf16), proj_embed, preferred_element_type=f32
    )
    spread = (ROWS, WIDE - KEYW)
    parts = jnp.concatenate(
        [
            part_hidden,
            jnp.broadcast_to(jnp.sum(hidden_wide * hidden_wide, axis=1, keepdims=True), spread),
            part_next,
            jnp.broadcast_to(jnp.sum(next_wide * next_wide, axis=1, keepdims=True), spread),
        ],
        axis=1,
    ).reshape(N_TP, PIECE, 2 * WIDE)
    parts = lax.all_to_all(parts, TP, split_axis=0, concat_axis=0, tiled=True)

    cos_table, sin_table = rotation(row_positions(ctx, jnp.arange(ROWS)))
    cos_table = cos_table.reshape(2, 1, HALF, ROPE // 2)
    sin_table = sin_table.reshape(2, 1, HALF, ROPE // 2)
    key_up_heads = key_up.reshape(LAT, HEADS, NOPE)
    value_up_heads = value_up.reshape(LAT, HEADS, VDIM)
    query_heads = queries.reshape(2, HALF, HEADS, NOPE + ROPE).transpose(0, 2, 1, 3)
    query_rot = rotate_pairs(query_heads[..., NOPE:].astype(f32), cos_table, sin_table)
    query_latent = jnp.einsum(
        "ghsn,lhn->ghsl", query_heads[..., :NOPE], key_up_heads, preferred_element_type=f32
    )
    q = jnp.concatenate([query_latent.astype(bf16), query_rot.astype(bf16)], axis=3)
    q = q.reshape(2, SEG, KEYW)
    g = jnp.einsum(
        "gshv,lhv->ghsl",
        grad_out.reshape(2, HALF, HEADS, VDIM),
        value_up_heads,
        preferred_element_type=f32,
    )
    g = g.astype(bf16).reshape(2, SEG, LAT)
    qt, gt = q.swapaxes(1, 2), g.swapaxes(1, 2)

    parts, q, qt, g, gt = lax.optimization_barrier((parts, q, qt, g, gt))
    parts = jnp.sum(parts, axis=0)
    part_hidden, part_next = parts[:, :KEYW], parts[:, WIDE : WIDE + KEYW]
    inv_hidden = lax.rsqrt(parts[:, KEYW : KEYW + 1] / D + EPSILON)
    inv_next = lax.rsqrt(parts[:, WIDE + KEYW : WIDE + KEYW + 1] / D + EPSILON)
    latent = inv_hidden * part_hidden + inv_next * part_next
    leading = latent[:, :LAT]
    inv_latent = lax.rsqrt(jnp.mean(leading * leading, axis=1, keepdims=True) + EPSILON)
    piece_cos, piece_sin = rotation(row_positions(ctx, tp * PIECE + jnp.arange(PIECE)))
    key_piece = jnp.concatenate(
        [
            (leading * inv_latent * gain_latent).astype(bf16),
            rotate_pairs(latent[:, LAT:], piece_cos, piece_sin).astype(bf16),
            jnp.zeros((PIECE, WIDE - KEYW), bf16),
        ],
        axis=1,
    )
    same = pack_keys(gather_copies(key_piece, XZ, 16).reshape(2, 128, WIDE))
    mine = gather_copies(same, TP, N_TP)
    other = lax.ppermute(mine, "co", [(0, 1), (1, 0)])

    where = jnp.stack([ctx, core]).astype(jnp.int32)
    ot, leadt, tailt, dmine, dother = attention(
        where, mine, other, q, qt, g, gt
    )

    received = lax.ppermute(dother, "co", [(0, 1), (1, 0)])
    dkey = (dmine.astype(f32) + received.astype(f32)).astype(bf16)
    dkey = lax.all_to_all(dkey, TP, split_axis=0, concat_axis=0, tiled=True)
    dkey = unpack_keys(jnp.sum(dkey.astype(f32), axis=0).astype(bf16)).reshape(16, PIECE, WIDE)
    dkey = lax.all_to_all(dkey, XZ, split_axis=0, concat_axis=0, tiled=True)
    dkey = jnp.sum(dkey.astype(f32), axis=0)[:, :KEYW]

    attended = jnp.einsum(
        "glhs,lhv->gshv",
        ot.reshape(2, LAT, HEADS, HALF),
        value_up_heads,
        preferred_element_type=f32,
    )
    attended = attended.astype(bf16).reshape(ROWS, HEADS * VDIM)
    grad_nope = jnp.einsum(
        "glhs,lhn->ghsn",
        leadt.reshape(2, LAT, HEADS, HALF),
        key_up_heads,
        preferred_element_type=f32,
    )
    grad_rope = unrotate(
        tailt.reshape(2, ROPE, HEADS, HALF).transpose(0, 2, 3, 1), cos_table, sin_table
    )
    grad_queries = jnp.concatenate([grad_nope, grad_rope], axis=3).astype(bf16)
    grad_queries = grad_queries.transpose(0, 2, 1, 3).reshape(ROWS, HEADS * (NOPE + ROPE))

    gained = gain_latent * dkey[:, :LAT]
    dlatent = jnp.concatenate(
        [
            inv_latent * gained
            - inv_latent**3 * leading * jnp.sum(gained * leading, axis=1, keepdims=True) / LAT,
            unrotate(dkey[:, LAT:], piece_cos, piece_sin),
        ],
        axis=1,
    )
    coef_hidden = jnp.sum(dlatent * part_hidden, axis=1, keepdims=True) * inv_hidden**3 / D
    coef_next = jnp.sum(dlatent * part_next, axis=1, keepdims=True) * inv_next**3 / D

    def in_two(c):
        high = c.astype(bf16)
        low = (c - high.astype(f32)).astype(bf16)
        width = (PIECE, (WIDE - KEYW) // 2)
        return [jnp.broadcast_to(high, width), jnp.broadcast_to(low, width)]

    packed = jnp.concatenate(
        [(inv_hidden * dlatent).astype(bf16)]
        + in_two(coef_hidden)
        + [(inv_next * dlatent).astype(bf16)]
        + in_two(coef_next),
        axis=1,
    )
    packed = gather_copies(packed, TP, N_TP).reshape(ROWS, 2 * WIDE)

    def whole(block):
        high = block[:, KEYW : KEYW + 1].astype(f32)
        return block[:, :KEYW], high + block[:, WIDE - 1 :].astype(f32)

    dpart_hidden, coef_hidden = whole(packed[:, :WIDE])
    grad_hidden = (
        gain_hidden
        * jnp.einsum("rc,dc->rd", dpart_hidden, proj_hidden, preferred_element_type=f32)
        - coef_hidden * hidden_wide
    ).astype(bf16)

    nexts = packed[:, WIDE:]
    after, before = edge_exchange(nexts[ROWS - 1 :], nexts[HALF - 1 : HALF])
    before_late = jnp.where(last, nexts[HALF - 1 : HALF], after)
    shifted = jnp.concatenate(
        [before, nexts[: HALF - 1], before_late, nexts[HALF : ROWS - 1]], axis=0
    )
    dpart_next, coef_next = whole(shifted)
    grad_embed = (
        gain_embed
        * jnp.einsum("rc,dc->rd", dpart_next, proj_embed, preferred_element_type=f32)
        - coef_next * embed.astype(f32)
    ).astype(bf16)
    return (attended, grad_queries, grad_hidden, grad_embed)


def solution(mesh):
    axes = ("xh", "z", "co", "xl", "y")
    fine = Mesh(mesh.devices.reshape(2, 8, 2, 2, 4), axes)
    both = P(CTX, TP)
    placed = (
        both,
        both,
        P(TP),
        P(TP),
        P(TP, None),
        P(TP, None),
        P(),
        P(None, TP),
        P(None, TP),
        both,
        both,
    )
    return jax.shard_map(
        on_device,
        mesh=fine,
        in_specs=placed,
        out_specs=(both, both, both, both),
        check_vma=False,
    )
```

```python
import functools

import jax
import jax.numpy as jnp
from jax import lax
from jax.experimental import pallas as pl
from jax.experimental.pallas import tpu as pltpu
from jax.sharding import Mesh, PartitionSpec as P

D = 7168
LAT = 512
ROPE = 64
NOPE = 128
VDIM = 128
KEYW = LAT + ROPE
WIDE = 640

EPSILON = 1e-06
ROTARY_BASE = 10000.0
SCALE = (NOPE + ROPE) ** (-0.5)
LOG2E = 1.4426950408889634

CTX = ("xh", "z", "co")
TP = ("xl", "y")
XZ = ("xh", "z")
N_CTX = 32
N_TP = 8
HEADS = 8
HALF = 64
ROWS = 128
PIECE = ROWS // N_TP
SEG = HALF * HEADS
BLOCK = 512
STEPS = 9

bf16 = jnp.bfloat16
f32 = jnp.float32


def rotation(positions):
    pair_count = ROPE // 2
    frequency = ROTARY_BASE ** (-jnp.arange(pair_count, dtype=f32) / pair_count)
    angles = positions.astype(f32)[:, None] * frequency[None, :]
    return (jnp.cos(angles), jnp.sin(angles))


def rotate_pairs(values, cos_table, sin_table):
    a, b = jnp.split(values, 2, axis=-1)
    return jnp.concatenate(
        [a * cos_table - b * sin_table, a * sin_table + b * cos_table], axis=-1
    )


def unrotate(values, cos_table, sin_table):
    a, b = jnp.split(values, 2, axis=-1)
    return jnp.concatenate(
        [a * cos_table + b * sin_table, b * cos_table - a * sin_table], axis=-1
    )


def row_positions(ctx, rows):
    return jnp.where(rows < HALF, ctx * HALF + rows, (63 - ctx) * HALF + rows - HALF)


def gather_copies(x, axes, n):
    copies = jnp.broadcast_to(x[None], (n, *x.shape))
    return lax.all_to_all(copies, axes, split_axis=0, concat_axis=0, tiled=True)


def edge_exchange(first_row, second_row):
    down = [(i + 1, i) for i in range(N_CTX - 1)]
    up = [(i, i + 1) for i in range(N_CTX - 1)]
    return lax.ppermute(first_row, CTX, down), lax.ppermute(second_row, CTX, up)


def pack_keys(rows):
    lead = rows[..., :LAT].reshape(2, 128, 4, 128).transpose(0, 2, 1, 3).reshape(8, 128, 128)
    rope = jnp.concatenate([rows[0, :, LAT:KEYW], rows[1, :, LAT:KEYW]], axis=1)
    return jnp.concatenate([lead, rope[None]], axis=0)


def merge_kernel(in_ref, out_ref):
    total = in_ref[0].astype(f32)
    for t in range(1, N_TP):
        total = total + in_ref[t].astype(f32)
    total = total.astype(bf16)
    for xh in range(2):
        rope = total[8, :, xh * ROPE : (xh + 1) * ROPE]
        row = jnp.concatenate(
            [total[xh * 4 + c] for c in range(4)] + [rope, jnp.zeros_like(rope)], axis=1
        )
        for z in range(8):
            out_ref[xh * 8 + z] = row[z * PIECE : (z + 1) * PIECE]


def merge(arrived):
    return pl.pallas_call(
        merge_kernel,
        out_shape=jax.ShapeDtypeStruct((16, PIECE, WIDE), bf16),
        compiler_params=pltpu.CompilerParams(vmem_limit_bytes=16 * 1024 * 1024),
        cost_estimate=pl.CostEstimate(
            flops=1_200_000, bytes_accessed=2_700_000, transcendentals=0
        ),
        name="merge",
    )(arrived)


def attention_kernel(
    where_ref,
    mine_ref,
    other_ref,
    q_hbm,
    qt_hbm,
    g_hbm,
    gt_hbm,
    ot_hbm,
    leadt_hbm,
    tailt_hbm,
    dmine_ref,
    dother_ref,
    keys,
    q_ref,
    qt_ref,
    g_ref,
    gt_ref,
    s_buf,
    dp_buf,
    m_buf,
    l_buf,
    a_buf,
    ot_buf,
    dqt_buf,
    ot_out,
    lead_out,
    dk_buf,
    dk_out,
    sems,
    out_sems,
):
    ctx = where_ref[0]
    core = where_ref[1]
    copies = [
        pltpu.make_async_copy(source, target, sems.at[n])
        for n, (source, target) in enumerate(
            [
                (mine_ref, keys.at[core]),
                (qt_hbm, qt_ref),
                (gt_hbm, gt_ref),
                (other_ref, keys.at[1 - core]),
                (q_hbm, q_ref),
                (g_hbm, g_ref),
            ]
        )
    ]
    for copy in copies:
        copy.start()
    m_buf[...] = jnp.full_like(m_buf, -jnp.inf)
    l_buf[...] = jnp.zeros_like(l_buf)
    a_buf[...] = jnp.zeros_like(a_buf)
    ot_buf[...] = jnp.zeros_like(ot_buf)
    dqt_buf[...] = jnp.zeros_like(dqt_buf)

    def clear(t, carry):
        dk_buf[0, t] = jnp.zeros((9, 128, 128), f32)
        dk_buf[1, t] = jnp.zeros((9, 128, 128), f32)
        return carry

    lax.fori_loop(0, N_TP, clear, 0)
    for copy in copies[:4]:
        copy.wait()

    group = ctx // 8
    early_steps = group + 1

    def locate(i):
        late = i >= early_steps
        j = i - early_steps
        half = jnp.logical_and(late, j >= 4).astype(jnp.int32)
        block = jnp.where(late, jnp.where(j >= 4, group + j - 4, j), i)
        return late.astype(jnp.int32), half, block

    def slab(half, block):
        xh = block // 2
        at = pl.multiple_of((block % 2) * 64, 64)

        def tile(part):
            return jnp.concatenate(
                [
                    keys[co, half * 4 + y, part, pl.ds(at, 64), :]
                    for co in range(2)
                    for y in range(4)
                ],
                axis=0,
            )

        rope = tile(8)
        rope = jnp.where(xh == 0, rope[:, :ROPE], rope[:, ROPE:])
        return jnp.concatenate([tile(xh * 4 + c) for c in range(4)] + [rope], axis=1)

    def nn(a, b):
        return jnp.dot(a, b, preferred_element_type=f32)

    def first(i, carry):
        seg, half, block = locate(i)
        k = slab(half, block)
        idx = lax.broadcasted_iota(jnp.int32, (BLOCK, 1), 0)
        owner = block * 8 + ((idx // 16) % 4) * 2 + idx // 256
        within = ((idx // 64) % 4) * 16 + idx % 16
        key_pos = jnp.where(half == 0, owner, 63 - owner) * 64 + within
        wide = SEG // 1
        row = lax.broadcasted_iota(jnp.int32, (1, wide), 1)
        q_pos = jnp.where(seg == 0, ctx, 63 - ctx) * 64 + row % 64
        for at in range(0, SEG, wide):
            part = slice(at, at + wide)
            s = nn(k, qt_ref[seg, :, part]) * (SCALE * LOG2E)
            s = jnp.where(key_pos <= q_pos, s, -jnp.inf)
            s_buf[i, :, part] = s
            dp = nn(k[:, :LAT], gt_ref[seg, :, part])
            dp_buf[i, :, part] = dp
            m_old = m_buf[seg, :, part]
            m_new = jnp.maximum(m_old, jnp.max(s, axis=0, keepdims=True))
            alpha = jnp.exp2(m_old - m_new)
            e = jnp.exp2(s - m_new)
            m_buf[seg, :, part] = m_new
            l_buf[seg, :, part] = l_buf[seg, :, part] * alpha + jnp.sum(e, axis=0, keepdims=True)
            a_buf[seg, :, part] = a_buf[seg, :, part] * alpha + jnp.sum(
                e * dp, axis=0, keepdims=True
            )
        return carry

    lax.fori_loop(0, STEPS, first, 0)
    for copy in copies[4:]:
        copy.wait()
    a_buf[...] = a_buf[...] / l_buf[...]
    m_buf[...] = m_buf[...] + jnp.log2(l_buf[...])

    def second(i, carry):
        seg, half, block = locate(i)
        k = slab(half, block)
        kt = k.T
        wide = SEG // 1
        lead = None
        for at in range(0, SEG, wide):
            part = slice(at, at + wide)
            p = jnp.exp2(s_buf[i, :, part] - m_buf[seg, :, part]).astype(bf16)
            ds = (p.astype(f32) * ((dp_buf[i, :, part] - a_buf[seg, :, part]) * SCALE)).astype(bf16)
            ot_buf[seg, :, part] += nn(kt[:LAT], p)
            dqt_buf[seg, :, part] += nn(kt, ds)
            more = nn(ds, q_ref[seg, part, :LAT]) + nn(p, g_ref[seg, part, :])
            rest = nn(ds, q_ref[seg, part, LAT:])
            lead = more if lead is None else lead + more
            tail = rest if at == 0 else tail + rest
        xh = block // 2
        at = pl.multiple_of((block % 2) * 64, 64)
        lane = lax.broadcasted_iota(jnp.int32, (1, 128), 1)
        tail = jnp.where(lane // ROPE == xh, jnp.concatenate([tail, tail], axis=1), 0.0)
        for co in range(2):
            for y in range(4):
                j = (co * 4 + y) * 64
                own = half * 4 + y
                for c in range(4):
                    dk_buf[co, own, xh * 4 + c, pl.ds(at, 64), :] += lead[
                        j : j + 64, c * 128 : c * 128 + 128
                    ]
                dk_buf[co, own, 8, pl.ds(at, 64), :] += tail[j : j + 64]
        return carry

    lax.fori_loop(0, STEPS, second, 0)

    sends = []

    def send(source, target):
        copy = pltpu.make_async_copy(source, target, out_sems.at[len(sends)])
        copy.start()
        sends.append(copy)

    send(dqt_buf.at[:, pl.ds(LAT, ROPE)], tailt_hbm)
    for t in range(N_TP):
        dk_out[0, t] = dk_buf[1 - core, t].astype(bf16)
        send(dk_out.at[0, t], dother_ref.at[t])
    for t in range(N_TP):
        dk_out[1, t] = dk_buf[core, t].astype(bf16)
        send(dk_out.at[1, t], dmine_ref.at[t])
    for seg in range(2):
        ot_out[seg] = ot_buf[seg].astype(bf16)
        send(ot_out.at[seg], ot_hbm.at[seg])
        lead_out[seg] = dqt_buf[seg, :LAT].astype(bf16)
        send(lead_out.at[seg], leadt_hbm.at[seg])
    for copy in sends:
        copy.wait()


def attention(where, mine, other, q, qt, g, gt):
    hbm = pl.BlockSpec(memory_space=pl.ANY)
    half_keys = (N_TP, 9, 128, 128)
    return pl.pallas_call(
        attention_kernel,
        in_specs=[pl.BlockSpec(memory_space=pltpu.SMEM)] + [hbm] * 6,
        out_specs=[hbm] * 5,
        out_shape=[
            jax.ShapeDtypeStruct((2, LAT, SEG), bf16),
            jax.ShapeDtypeStruct((2, LAT, SEG), bf16),
            jax.ShapeDtypeStruct((2, ROPE, SEG), f32),
            jax.ShapeDtypeStruct(half_keys, bf16),
            jax.ShapeDtypeStruct(half_keys, bf16),
        ],
        scratch_shapes=[
            pltpu.VMEM((2,) + half_keys, bf16),
            pltpu.VMEM((2, SEG, KEYW), bf16),
            pltpu.VMEM((2, KEYW, SEG), bf16),
            pltpu.VMEM((2, SEG, LAT), bf16),
            pltpu.VMEM((2, LAT, SEG), bf16),
            pltpu.VMEM((STEPS, BLOCK, SEG), f32),
            pltpu.VMEM((STEPS, BLOCK, SEG), f32),
            pltpu.VMEM((2, 1, SEG), f32),
            pltpu.VMEM((2, 1, SEG), f32),
            pltpu.VMEM((2, 1, SEG), f32),
            pltpu.VMEM((2, LAT, SEG), f32),
            pltpu.VMEM((2, KEYW, SEG), f32),
            pltpu.VMEM((2, LAT, SEG), bf16),
            pltpu.VMEM((2, LAT, SEG), bf16),
            pltpu.VMEM((2,) + half_keys, f32),
            pltpu.VMEM((2,) + half_keys, bf16),
            pltpu.SemaphoreType.DMA((6,)),
            pltpu.SemaphoreType.DMA((21,)),
        ],
        compiler_params=pltpu.CompilerParams(vmem_limit_bytes=58 * 1024 * 1024),
        cost_estimate=pl.CostEstimate(
            flops=14_000_000_000, bytes_accessed=20_000_000, transcendentals=4_000_000
        ),
        name="attention",
    )(where, mine, other, q, qt, g, gt)


def on_device(
    hidden,
    embed,
    gain_hidden,
    gain_embed,
    proj_hidden,
    proj_embed,
    gain_latent,
    key_up,
    value_up,
    queries,
    grad_out,
):
    ctx = lax.axis_index(CTX)
    core = lax.axis_index("co")
    tp = lax.axis_index(TP)
    last = ctx == N_CTX - 1

    after, before = edge_exchange(embed[0:1], embed[HALF : HALF + 1])
    after_early = jnp.where(last, embed[HALF : HALF + 1], after)
    next_embed = jnp.concatenate(
        [embed[1:HALF], after_early, embed[HALF + 1 :], before], axis=0
    )
    hidden_wide = hidden.astype(f32)
    next_wide = next_embed.astype(f32)
    part_hidden = jnp.dot(
        (hidden_wide * gain_hidden).astype(bf16), proj_hidden, preferred_element_type=f32
    )
    part_next = jnp.dot(
        (next_wide * gain_embed).astype(bf16), proj_embed, preferred_element_type=f32
    )
    spread = (ROWS, WIDE - KEYW)
    parts = jnp.concatenate(
        [
            part_hidden,
            jnp.broadcast_to(jnp.sum(hidden_wide * hidden_wide, axis=1, keepdims=True), spread),
            part_next,
            jnp.broadcast_to(jnp.sum(next_wide * next_wide, axis=1, keepdims=True), spread),
        ],
        axis=1,
    ).reshape(N_TP, PIECE, 2 * WIDE)
    parts = lax.all_to_all(parts, TP, split_axis=0, concat_axis=0, tiled=True)

    parts, queries, grad_out = lax.optimization_barrier((parts, queries, grad_out))
    parts = jnp.sum(parts, axis=0)
    part_hidden, part_next = parts[:, :KEYW], parts[:, WIDE : WIDE + KEYW]
    inv_hidden = lax.rsqrt(parts[:, KEYW : KEYW + 1] / D + EPSILON)
    inv_next = lax.rsqrt(parts[:, WIDE + KEYW : WIDE + KEYW + 1] / D + EPSILON)
    latent = inv_hidden * part_hidden + inv_next * part_next
    leading = latent[:, :LAT]
    inv_latent = lax.rsqrt(jnp.mean(leading * leading, axis=1, keepdims=True) + EPSILON)
    piece_cos, piece_sin = rotation(row_positions(ctx, tp * PIECE + jnp.arange(PIECE)))
    key_piece = jnp.concatenate(
        [
            (leading * inv_latent * gain_latent).astype(bf16),
            rotate_pairs(latent[:, LAT:], piece_cos, piece_sin).astype(bf16),
            jnp.zeros((PIECE, WIDE - KEYW), bf16),
        ],
        axis=1,
    )
    same = pack_keys(gather_copies(key_piece, XZ, 16).reshape(2, 128, WIDE))
    mine = gather_copies(same, TP, N_TP)

    cos_table, sin_table = rotation(row_positions(ctx, jnp.arange(ROWS)))
    cos_table = cos_table.reshape(2, 1, HALF, ROPE // 2)
    sin_table = sin_table.reshape(2, 1, HALF, ROPE // 2)
    key_up_heads = key_up.reshape(LAT, HEADS, NOPE)
    value_up_heads = value_up.reshape(LAT, HEADS, VDIM)
    query_heads = queries.reshape(2, HALF, HEADS, NOPE + ROPE).transpose(0, 2, 1, 3)
    query_rot = rotate_pairs(query_heads[..., NOPE:].astype(f32), cos_table, sin_table)
    query_latent = jnp.einsum(
        "ghsn,lhn->ghsl", query_heads[..., :NOPE], key_up_heads, preferred_element_type=f32
    )
    q = jnp.concatenate([query_latent.astype(bf16), query_rot.astype(bf16)], axis=3)
    q = q.reshape(2, SEG, KEYW)
    g = jnp.einsum(
        "gshv,lhv->ghsl",
        grad_out.reshape(2, HALF, HEADS, VDIM),
        value_up_heads,
        preferred_element_type=f32,
    )
    g = g.astype(bf16).reshape(2, SEG, LAT)
    qt, gt = q.swapaxes(1, 2), g.swapaxes(1, 2)
    mine, q, qt, g, gt = lax.optimization_barrier((mine, q, qt, g, gt))
    other = lax.ppermute(mine, "co", [(0, 1), (1, 0)])

    where = jnp.stack([ctx, core]).astype(jnp.int32)
    ot, leadt, tailt, dmine, dother = attention(
        where, mine, other, q, qt, g, gt
    )

    received = lax.ppermute(dother, "co", [(0, 1), (1, 0)])
    dkey = (dmine.astype(f32) + received.astype(f32)).astype(bf16)
    dkey = lax.all_to_all(dkey, TP, split_axis=0, concat_axis=0, tiled=True)

    attended = jnp.einsum(
        "glhs,lhv->gshv",
        ot.reshape(2, LAT, HEADS, HALF),
        value_up_heads,
        preferred_element_type=f32,
    )
    attended = attended.astype(bf16).reshape(ROWS, HEADS * VDIM)
    grad_nope = jnp.einsum(
        "glhs,lhn->ghsn",
        leadt.reshape(2, LAT, HEADS, HALF),
        key_up_heads,
        preferred_element_type=f32,
    )
    grad_rope = unrotate(
        tailt.reshape(2, ROPE, HEADS, HALF).transpose(0, 2, 3, 1), cos_table, sin_table
    )
    grad_queries = jnp.concatenate([grad_nope, grad_rope], axis=3).astype(bf16)
    grad_queries = grad_queries.transpose(0, 2, 1, 3).reshape(ROWS, HEADS * (NOPE + ROPE))
    dkey, attended, grad_queries = lax.optimization_barrier((dkey, attended, grad_queries))

    dkey = lax.all_to_all(merge(dkey), XZ, split_axis=0, concat_axis=0, tiled=True)
    dkey = jnp.sum(dkey.astype(f32), axis=0)[:, :KEYW]

    gained = gain_latent * dkey[:, :LAT]
    dlatent = jnp.concatenate(
        [
            inv_latent * gained
            - inv_latent**3 * leading * jnp.sum(gained * leading, axis=1, keepdims=True) / LAT,
            unrotate(dkey[:, LAT:], piece_cos, piece_sin),
        ],
        axis=1,
    )
    coef_hidden = jnp.sum(dlatent * part_hidden, axis=1, keepdims=True) * inv_hidden**3 / D
    coef_next = jnp.sum(dlatent * part_next, axis=1, keepdims=True) * inv_next**3 / D

    def in_two(c):
        high = c.astype(bf16)
        low = (c - high.astype(f32)).astype(bf16)
        width = (PIECE, (WIDE - KEYW) // 2)
        return [jnp.broadcast_to(high, width), jnp.broadcast_to(low, width)]

    packed = jnp.concatenate(
        [(inv_hidden * dlatent).astype(bf16)]
        + in_two(coef_hidden)
        + [(inv_next * dlatent).astype(bf16)]
        + in_two(coef_next),
        axis=1,
    )
    packed = gather_copies(packed, TP, N_TP).reshape(ROWS, 2 * WIDE)

    def whole(block):
        high = block[:, KEYW : KEYW + 1].astype(f32)
        return block[:, :KEYW], high + block[:, WIDE - 1 :].astype(f32)

    dpart_hidden, coef_hidden = whole(packed[:, :WIDE])
    grad_hidden = (
        gain_hidden
        * jnp.einsum("rc,dc->rd", dpart_hidden, proj_hidden, preferred_element_type=f32)
        - coef_hidden * hidden_wide
    ).astype(bf16)

    nexts = packed[:, WIDE:]
    after, before = edge_exchange(nexts[ROWS - 1 :], nexts[HALF - 1 : HALF])
    before_late = jnp.where(last, nexts[HALF - 1 : HALF], after)
    shifted = jnp.concatenate(
        [before, nexts[: HALF - 1], before_late, nexts[HALF : ROWS - 1]], axis=0
    )
    dpart_next, coef_next = whole(shifted)
    grad_embed = (
        gain_embed
        * jnp.einsum("rc,dc->rd", dpart_next, proj_embed, preferred_element_type=f32)
        - coef_next * embed.astype(f32)
    ).astype(bf16)
    return (attended, grad_queries, grad_hidden, grad_embed)


def solution(mesh):
    axes = ("xh", "z", "co", "xl", "y")
    fine = Mesh(mesh.devices.reshape(2, 8, 2, 2, 4), axes)
    both = P(CTX, TP)
    placed = (
        both,
        both,
        P(TP),
        P(TP),
        P(TP, None),
        P(TP, None),
        P(),
        P(None, TP),
        P(None, TP),
        both,
        both,
    )
    return jax.shard_map(
        on_device,
        mesh=fine,
        in_specs=placed,
        out_specs=(both, both, both, both),
        check_vma=False,
    )
```

```python
import functools

import jax
import jax.numpy as jnp
from jax import lax
from jax.experimental import pallas as pl
from jax.experimental.pallas import tpu as pltpu
from jax.sharding import Mesh, PartitionSpec as P

D = 7168
LAT = 512
ROPE = 64
NOPE = 128
VDIM = 128
KEYW = LAT + ROPE
WIDE = 640

EPSILON = 1e-06
ROTARY_BASE = 10000.0
SCALE = (NOPE + ROPE) ** (-0.5)
LOG2E = 1.4426950408889634

CTX = ("xh", "z", "co")
TP = ("xl", "y")
XY = ("xh", "xl", "y")
N_CTX = 32
N_TP = 8
N_Z = 8
N_XY = 16
HEADS = 8
HALF = 64
ROWS = 128
PIECE = ROWS // N_TP
SEG = HALF * HEADS
BLOCK = 512
STEPS = 9

ALL = CTX + TP
ORDER = [c * N_TP + t for c in range(N_CTX) for t in range(N_TP // 2)] + [
    c * N_TP + t for c in reversed(range(N_CTX)) for t in range(N_TP // 2, N_TP)
]

bf16 = jnp.bfloat16
f32 = jnp.float32


def rotation(positions):
    pair_count = ROPE // 2
    frequency = ROTARY_BASE ** (-jnp.arange(pair_count, dtype=f32) / pair_count)
    angles = positions.astype(f32)[:, None] * frequency[None, :]
    return (jnp.cos(angles), jnp.sin(angles))


def rotate_pairs(values, cos_table, sin_table):
    a, b = jnp.split(values, 2, axis=-1)
    return jnp.concatenate(
        [a * cos_table - b * sin_table, a * sin_table + b * cos_table], axis=-1
    )


def unrotate(values, cos_table, sin_table):
    a, b = jnp.split(values, 2, axis=-1)
    return jnp.concatenate(
        [a * cos_table + b * sin_table, b * cos_table - a * sin_table], axis=-1
    )


def row_positions(ctx, rows):
    return jnp.where(rows < HALF, ctx * HALF + rows, (63 - ctx) * HALF + rows - HALF)


def gather_copies(x, axes, n):
    copies = jnp.broadcast_to(x[None], (n, *x.shape))
    return lax.all_to_all(copies, axes, split_axis=0, concat_axis=0, tiled=True)


def pack_keys(rows):
    lead = rows[:, :LAT].reshape(2, 64, 4, 128).transpose(0, 2, 1, 3).reshape(8, 64, 128)
    rope = jnp.concatenate([rows[:64, LAT:KEYW], rows[64:, LAT:KEYW]], axis=1)
    return jnp.concatenate([lead, rope[None]], axis=0)


def merge_kernel(in_ref, out_ref):
    total = in_ref[0].astype(f32)
    for t in range(1, N_XY):
        total = total + in_ref[t].astype(f32)
    total = total.astype(bf16)
    for zh in range(2):
        rope = total[8, :, zh * ROPE : (zh + 1) * ROPE]
        row = jnp.concatenate(
            [total[zh * 4 + c] for c in range(4)] + [rope, jnp.zeros_like(rope)], axis=1
        )
        for z in range(4):
            out_ref[zh * 4 + z] = row[z * PIECE : (z + 1) * PIECE]


def merge(arrived):
    return pl.pallas_call(
        merge_kernel,
        out_shape=jax.ShapeDtypeStruct((N_Z, PIECE, WIDE), bf16),
        compiler_params=pltpu.CompilerParams(vmem_limit_bytes=16 * 1024 * 1024),
        cost_estimate=pl.CostEstimate(
            flops=1_200_000, bytes_accessed=2_500_000, transcendentals=0
        ),
        name="merge",
    )(arrived)


def add_kernel(a_ref, b_ref, out_ref):
    out_ref[...] = (a_ref[...].astype(f32) + b_ref[...].astype(f32)).astype(bf16)


def add_cores(mine, received):
    block = pl.BlockSpec((2, 9, 64, 128), lambda i: (i, 0, 0, 0))
    return pl.pallas_call(
        add_kernel,
        grid=(N_XY // 2,),
        in_specs=[block, block],
        out_specs=block,
        out_shape=jax.ShapeDtypeStruct(mine.shape, bf16),
        cost_estimate=pl.CostEstimate(
            flops=1_200_000, bytes_accessed=7_100_000, transcendentals=0
        ),
        name="add_cores",
    )(mine, received)


def attention_kernel(
    where_ref,
    mine_ref,
    other_ref,
    q_hbm,
    qt_hbm,
    g_hbm,
    gt_hbm,
    ot_hbm,
    leadt_hbm,
    tailt_hbm,
    dmine_ref,
    dother_ref,
    keys,
    q_ref,
    qt_ref,
    g_ref,
    gt_ref,
    s_buf,
    dp_buf,
    m_buf,
    l_buf,
    a_buf,
    ot_buf,
    dqt_buf,
    ot_out,
    lead_out,
    dk_buf,
    dk_out,
    sems,
    out_sems,
):
    ctx = where_ref[0]
    core = where_ref[1]
    copies = [
        pltpu.make_async_copy(source, target, sems.at[n])
        for n, (source, target) in enumerate(
            [
                (mine_ref, keys.at[core]),
                (qt_hbm, qt_ref),
                (gt_hbm, gt_ref),
                (other_ref, keys.at[1 - core]),
                (q_hbm, q_ref),
                (g_hbm, g_ref),
            ]
        )
    ]
    for copy in copies:
        copy.start()
    m_buf[...] = jnp.full_like(m_buf, -jnp.inf)
    l_buf[...] = jnp.zeros_like(l_buf)
    a_buf[...] = jnp.zeros_like(a_buf)
    ot_buf[...] = jnp.zeros_like(ot_buf)
    dqt_buf[...] = jnp.zeros_like(dqt_buf)

    def clear(t, carry):
        dk_buf[0, t] = jnp.zeros((9, 64, 128), f32)
        dk_buf[1, t] = jnp.zeros((9, 64, 128), f32)
        return carry

    lax.fori_loop(0, N_XY, clear, 0)
    for copy in copies[:4]:
        copy.wait()

    group = ctx // 8
    early_steps = group + 1

    def locate(i):
        late = i >= early_steps
        j = i - early_steps
        half = jnp.logical_and(late, j >= 4).astype(jnp.int32)
        block = jnp.where(late, jnp.where(j >= 4, group + j - 4, j), i)
        return late.astype(jnp.int32), half, block

    def slab(half, block):
        x4 = (block // 2 * 2 + half) * 4
        zh = block % 2

        def tile(part):
            return jnp.concatenate(
                [keys[co, x4 + y, part] for co in range(2) for y in range(4)], axis=0
            )

        rope = tile(8)
        rope = jnp.where(zh == 0, rope[:, :ROPE], rope[:, ROPE:])
        return jnp.concatenate([tile(zh * 4 + c) for c in range(4)] + [rope], axis=1)

    def nn(a, b):
        return jnp.dot(a, b, preferred_element_type=f32)

    def first(i, carry):
        seg, half, block = locate(i)
        k = slab(half, block)
        idx = lax.broadcasted_iota(jnp.int32, (BLOCK, 1), 0)
        owner = block * 8 + ((idx // 16) % 4) * 2 + idx // 256
        within = ((idx // 64) % 4) * 16 + idx % 16
        key_pos = jnp.where(half == 0, owner, 63 - owner) * 64 + within
        wide = SEG // 1
        row = lax.broadcasted_iota(jnp.int32, (1, wide), 1)
        q_pos = jnp.where(seg == 0, ctx, 63 - ctx) * 64 + row % 64
        for at in range(0, SEG, wide):
            part = slice(at, at + wide)
            s = nn(k, qt_ref[seg, :, part]) * (SCALE * LOG2E)
            s = jnp.where(key_pos <= q_pos, s, -jnp.inf)
            s_buf[i, :, part] = s
            dp = nn(k[:, :LAT], gt_ref[seg, :, part])
            dp_buf[i, :, part] = dp
            m_old = m_buf[seg, :, part]
            m_new = jnp.maximum(m_old, jnp.max(s, axis=0, keepdims=True))
            alpha = jnp.exp2(m_old - m_new)
            e = jnp.exp2(s - m_new)
            m_buf[seg, :, part] = m_new
            l_buf[seg, :, part] = l_buf[seg, :, part] * alpha + jnp.sum(e, axis=0, keepdims=True)
            a_buf[seg, :, part] = a_buf[seg, :, part] * alpha + jnp.sum(
                e * dp, axis=0, keepdims=True
            )
        return carry

    lax.fori_loop(0, STEPS, first, 0)
    for copy in copies[4:]:
        copy.wait()
    a_buf[...] = a_buf[...] / l_buf[...]
    m_buf[...] = m_buf[...] + jnp.log2(l_buf[...])

    def second(i, carry):
        seg, half, block = locate(i)
        k = slab(half, block)
        kt = k.T
        wide = SEG // 1
        lead = None
        for at in range(0, SEG, wide):
            part = slice(at, at + wide)
            p = jnp.exp2(s_buf[i, :, part] - m_buf[seg, :, part]).astype(bf16)
            ds = (p.astype(f32) * ((dp_buf[i, :, part] - a_buf[seg, :, part]) * SCALE)).astype(bf16)
            ot_buf[seg, :, part] += nn(kt[:LAT], p)
            dqt_buf[seg, :, part] += nn(kt, ds)
            more = nn(ds, q_ref[seg, part, :LAT]) + nn(p, g_ref[seg, part, :])
            rest = nn(ds, q_ref[seg, part, LAT:])
            lead = more if lead is None else lead + more
            tail = rest if at == 0 else tail + rest
        x4 = (block // 2 * 2 + half) * 4
        zh = block % 2
        lane = lax.broadcasted_iota(jnp.int32, (1, 128), 1)
        tail = jnp.where(lane // ROPE == zh, jnp.concatenate([tail, tail], axis=1), 0.0)
        for co in range(2):
            for y in range(4):
                j = (co * 4 + y) * 64
                for c in range(4):
                    dk_buf[co, x4 + y, zh * 4 + c] += lead[j : j + 64, c * 128 : c * 128 + 128]
                dk_buf[co, x4 + y, 8] += tail[j : j + 64]
        return carry

    lax.fori_loop(0, STEPS, second, 0)

    sends = []

    def send(source, target):
        copy = pltpu.make_async_copy(source, target, out_sems.at[len(sends)])
        copy.start()
        sends.append(copy)

    send(dqt_buf.at[:, pl.ds(LAT, ROPE)], tailt_hbm)
    for t in range(0, N_XY, 2):
        dk_out[0, t : t + 2] = dk_buf[1 - core, t : t + 2].astype(bf16)
        send(dk_out.at[0, pl.ds(t, 2)], dother_ref.at[pl.ds(t, 2)])
    for t in range(0, N_XY, 2):
        dk_out[1, t : t + 2] = dk_buf[core, t : t + 2].astype(bf16)
        send(dk_out.at[1, pl.ds(t, 2)], dmine_ref.at[pl.ds(t, 2)])
    for seg in range(2):
        ot_out[seg] = ot_buf[seg].astype(bf16)
        send(ot_out.at[seg], ot_hbm.at[seg])
        lead_out[seg] = dqt_buf[seg, :LAT].astype(bf16)
        send(lead_out.at[seg], leadt_hbm.at[seg])
    for copy in sends:
        copy.wait()


def attention(where, mine, other, q, qt, g, gt):
    hbm = pl.BlockSpec(memory_space=pl.ANY)
    half_keys = (N_XY, 9, 64, 128)
    return pl.pallas_call(
        attention_kernel,
        in_specs=[pl.BlockSpec(memory_space=pltpu.SMEM)] + [hbm] * 6,
        out_specs=[hbm] * 5,
        out_shape=[
            jax.ShapeDtypeStruct((2, LAT, SEG), bf16),
            jax.ShapeDtypeStruct((2, LAT, SEG), bf16),
            jax.ShapeDtypeStruct((2, ROPE, SEG), f32),
            jax.ShapeDtypeStruct(half_keys, bf16),
            jax.ShapeDtypeStruct(half_keys, bf16),
        ],
        scratch_shapes=[
            pltpu.VMEM((2,) + half_keys, bf16),
            pltpu.VMEM((2, SEG, KEYW), bf16),
            pltpu.VMEM((2, KEYW, SEG), bf16),
            pltpu.VMEM((2, SEG, LAT), bf16),
            pltpu.VMEM((2, LAT, SEG), bf16),
            pltpu.VMEM((STEPS, BLOCK, SEG), f32),
            pltpu.VMEM((STEPS, BLOCK, SEG), f32),
            pltpu.VMEM((2, 1, SEG), f32),
            pltpu.VMEM((2, 1, SEG), f32),
            pltpu.VMEM((2, 1, SEG), f32),
            pltpu.VMEM((2, LAT, SEG), f32),
            pltpu.VMEM((2, KEYW, SEG), f32),
            pltpu.VMEM((2, LAT, SEG), bf16),
            pltpu.VMEM((2, LAT, SEG), bf16),
            pltpu.VMEM((2,) + half_keys, f32),
            pltpu.VMEM((2,) + half_keys, bf16),
            pltpu.SemaphoreType.DMA((6,)),
            pltpu.SemaphoreType.DMA((21,)),
        ],
        compiler_params=pltpu.CompilerParams(vmem_limit_bytes=60 * 1024 * 1024),
        cost_estimate=pl.CostEstimate(
            flops=14_000_000_000, bytes_accessed=20_000_000, transcendentals=4_000_000
        ),
        name="attention",
    )(where, mine, other, q, qt, g, gt)


def on_device(
    hidden,
    embed,
    gain_hidden,
    gain_embed,
    proj_hidden,
    proj_embed,
    gain_latent,
    key_up,
    value_up,
    queries,
    grad_out,
):
    ctx = lax.axis_index(CTX)
    core = lax.axis_index("co")
    tp = lax.axis_index(TP)

    hidden_wide = hidden.astype(f32)
    embed_wide = embed.astype(f32)
    part_hidden = jnp.dot(
        (hidden_wide * gain_hidden).astype(bf16), proj_hidden, preferred_element_type=f32
    )
    part_embed = jnp.dot(
        (embed_wide * gain_embed).astype(bf16), proj_embed, preferred_element_type=f32
    )
    spread = (ROWS, WIDE - KEYW)
    parts = jnp.concatenate(
        [
            part_hidden,
            jnp.broadcast_to(jnp.sum(hidden_wide * hidden_wide, axis=1, keepdims=True), spread),
            part_embed,
            jnp.broadcast_to(jnp.sum(embed_wide * embed_wide, axis=1, keepdims=True), spread),
        ],
        axis=1,
    ).reshape(N_TP, PIECE, 2 * WIDE)
    parts = lax.all_to_all(parts, TP, split_axis=0, concat_axis=0, tiled=True)

    parts, queries, grad_out = lax.optimization_barrier((parts, queries, grad_out))
    parts = jnp.sum(parts, axis=0)
    nexts = parts[:, WIDE:]
    after = lax.ppermute(nexts[:1], ALL, [(b, a) for a, b in zip(ORDER[:-1], ORDER[1:])])
    nexts = jnp.concatenate([nexts[1:], after], axis=0)
    part_hidden, part_next = parts[:, :KEYW], nexts[:, :KEYW]
    inv_hidden = lax.rsqrt(parts[:, KEYW : KEYW + 1] / D + EPSILON)
    inv_next = lax.rsqrt(nexts[:, KEYW : KEYW + 1] / D + EPSILON)
    latent = inv_hidden * part_hidden + inv_next * part_next
    leading = latent[:, :LAT]
    inv_latent = lax.rsqrt(jnp.mean(leading * leading, axis=1, keepdims=True) + EPSILON)
    piece_cos, piece_sin = rotation(row_positions(ctx, tp * PIECE + jnp.arange(PIECE)))
    key_piece = jnp.concatenate(
        [
            (leading * inv_latent * gain_latent).astype(bf16),
            rotate_pairs(latent[:, LAT:], piece_cos, piece_sin).astype(bf16),
            jnp.zeros((PIECE, WIDE - KEYW), bf16),
        ],
        axis=1,
    )
    same = pack_keys(gather_copies(key_piece, "z", N_Z).reshape(128, WIDE))
    mine = gather_copies(same, XY, N_XY)

    cos_table, sin_table = rotation(row_positions(ctx, jnp.arange(ROWS)))
    cos_table = cos_table.reshape(2, 1, HALF, ROPE // 2)
    sin_table = sin_table.reshape(2, 1, HALF, ROPE // 2)
    key_up_heads = key_up.reshape(LAT, HEADS, NOPE)
    value_up_heads = value_up.reshape(LAT, HEADS, VDIM)
    query_heads = queries.reshape(2, HALF, HEADS, NOPE + ROPE).transpose(0, 2, 1, 3)
    query_rot = rotate_pairs(query_heads[..., NOPE:].astype(f32), cos_table, sin_table)
    query_latent = jnp.einsum(
        "ghsn,lhn->ghsl", query_heads[..., :NOPE], key_up_heads, preferred_element_type=f32
    )
    q = jnp.concatenate([query_latent.astype(bf16), query_rot.astype(bf16)], axis=3)
    q = q.reshape(2, SEG, KEYW)
    g = jnp.einsum(
        "gshv,lhv->ghsl",
        grad_out.reshape(2, HALF, HEADS, VDIM),
        value_up_heads,
        preferred_element_type=f32,
    )
    g = g.astype(bf16).reshape(2, SEG, LAT)
    qt, gt = q.swapaxes(1, 2), g.swapaxes(1, 2)
    mine, q, qt, g, gt = lax.optimization_barrier((mine, q, qt, g, gt))
    other = lax.ppermute(mine, "co", [(0, 1), (1, 0)])

    where = jnp.stack([ctx, core]).astype(jnp.int32)
    ot, leadt, tailt, dmine, dother = attention(
        where, mine, other, q, qt, g, gt
    )

    received = lax.ppermute(dother, "co", [(0, 1), (1, 0)])
    dkey = add_cores(dmine, received)
    dkey = lax.all_to_all(dkey, XY, split_axis=0, concat_axis=0, tiled=True)

    attended = jnp.einsum(
        "glhs,lhv->gshv",
        ot.reshape(2, LAT, HEADS, HALF),
        value_up_heads,
        preferred_element_type=f32,
    )
    attended = attended.astype(bf16).reshape(ROWS, HEADS * VDIM)
    grad_nope = jnp.einsum(
        "glhs,lhn->ghsn",
        leadt.reshape(2, LAT, HEADS, HALF),
        key_up_heads,
        preferred_element_type=f32,
    )
    grad_rope = unrotate(
        tailt.reshape(2, ROPE, HEADS, HALF).transpose(0, 2, 3, 1), cos_table, sin_table
    )
    grad_queries = jnp.concatenate([grad_nope, grad_rope], axis=3).astype(bf16)
    grad_queries = grad_queries.transpose(0, 2, 1, 3).reshape(ROWS, HEADS * (NOPE + ROPE))
    dkey, attended, grad_queries = lax.optimization_barrier((dkey, attended, grad_queries))

    dkey = lax.all_to_all(merge(dkey), "z", split_axis=0, concat_axis=0, tiled=True)
    dkey = jnp.sum(dkey.astype(f32), axis=0)[:, :KEYW]

    gained = gain_latent * dkey[:, :LAT]
    dlatent = jnp.concatenate(
        [
            inv_latent * gained
            - inv_latent**3 * leading * jnp.sum(gained * leading, axis=1, keepdims=True) / LAT,
            unrotate(dkey[:, LAT:], piece_cos, piece_sin),
        ],
        axis=1,
    )
    coef_hidden = jnp.sum(dlatent * part_hidden, axis=1, keepdims=True) * inv_hidden**3 / D
    coef_next = jnp.sum(dlatent * part_next, axis=1, keepdims=True) * inv_next**3 / D

    def in_two(c):
        high = c.astype(bf16)
        low = (c - high.astype(f32)).astype(bf16)
        width = (PIECE, (WIDE - KEYW) // 2)
        return [jnp.broadcast_to(high, width), jnp.broadcast_to(low, width)]

    packed_hidden = jnp.concatenate(
        [(inv_hidden * dlatent).astype(bf16)] + in_two(coef_hidden), axis=1
    )
    packed_next = jnp.concatenate(
        [(inv_next * dlatent).astype(bf16)] + in_two(coef_next), axis=1
    )
    before = lax.ppermute(packed_next[-1:], ALL, list(zip(ORDER[:-1], ORDER[1:])))
    packed = jnp.concatenate(
        [packed_hidden, jnp.concatenate([before, packed_next[:-1]], axis=0)], axis=1
    )
    packed = gather_copies(packed, TP, N_TP).reshape(ROWS, 2 * WIDE)

    def whole(block):
        high = block[:, KEYW : KEYW + 1].astype(f32)
        return block[:, :KEYW], high + block[:, WIDE - 1 :].astype(f32)

    dpart_hidden, coef_hidden = whole(packed[:, :WIDE])
    grad_hidden = (
        gain_hidden
        * jnp.einsum("rc,dc->rd", dpart_hidden, proj_hidden, preferred_element_type=f32)
        - coef_hidden * hidden_wide
    ).astype(bf16)

    dpart_next, coef_next = whole(packed[:, WIDE:])
    grad_embed = (
        gain_embed
        * jnp.einsum("rc,dc->rd", dpart_next, proj_embed, preferred_element_type=f32)
        - coef_next * embed_wide
    ).astype(bf16)
    return (attended, grad_queries, grad_hidden, grad_embed)


def solution(mesh):
    axes = ("xh", "z", "co", "xl", "y")
    fine = Mesh(mesh.devices.reshape(2, 8, 2, 2, 4), axes)
    both = P(CTX, TP)
    placed = (
        both,
        both,
        P(TP),
        P(TP),
        P(TP, None),
        P(TP, None),
        P(),
        P(None, TP),
        P(None, TP),
        both,
        both,
    )
    return jax.shard_map(
        on_device,
        mesh=fine,
        in_specs=placed,
        out_specs=(both, both, both, both),
        check_vma=False,
    )
```

```python
import functools

import jax
import jax.numpy as jnp
from jax import lax
from jax.experimental import pallas as pl
from jax.experimental.pallas import tpu as pltpu
from jax.sharding import Mesh, PartitionSpec as P

D = 7168
LAT = 512
ROPE = 64
NOPE = 128
VDIM = 128
KEYW = LAT + ROPE
WIDE = 640

EPSILON = 1e-06
ROTARY_BASE = 10000.0
SCALE = (NOPE + ROPE) ** (-0.5)
LOG2E = 1.4426950408889634

CTX = ("xh", "z", "co")
TP = ("xl", "y")
XZ = ("xh", "z")
XY = ("xh", "xl", "y")
N_CTX = 32
N_TP = 8
N_Z = 8
N_XY = 16
HEADS = 8
HALF = 64
ROWS = 128
PIECE = ROWS // N_TP
SEG = HALF * HEADS
BLOCK = 512
STEPS = 9

ALL = CTX + TP
ORDER = [c * N_TP + t for c in range(N_CTX) for t in range(N_TP // 2)] + [
    c * N_TP + t for c in reversed(range(N_CTX)) for t in range(N_TP // 2, N_TP)
]

bf16 = jnp.bfloat16
f32 = jnp.float32


def rotation(positions):
    pair_count = ROPE // 2
    frequency = ROTARY_BASE ** (-jnp.arange(pair_count, dtype=f32) / pair_count)
    angles = positions.astype(f32)[:, None] * frequency[None, :]
    return (jnp.cos(angles), jnp.sin(angles))


def rotate_pairs(values, cos_table, sin_table):
    a, b = jnp.split(values, 2, axis=-1)
    return jnp.concatenate(
        [a * cos_table - b * sin_table, a * sin_table + b * cos_table], axis=-1
    )


def unrotate(values, cos_table, sin_table):
    a, b = jnp.split(values, 2, axis=-1)
    return jnp.concatenate(
        [a * cos_table + b * sin_table, b * cos_table - a * sin_table], axis=-1
    )


def row_positions(ctx, rows):
    return jnp.where(rows < HALF, ctx * HALF + rows, (63 - ctx) * HALF + rows - HALF)


def gather_copies(x, axes, n):
    copies = jnp.broadcast_to(x[None], (n, *x.shape))
    return lax.all_to_all(copies, axes, split_axis=0, concat_axis=0, tiled=True)


def edge_exchange(first_row, second_row):
    down = [(i + 1, i) for i in range(N_CTX - 1)]
    up = [(i, i + 1) for i in range(N_CTX - 1)]
    return lax.ppermute(first_row, CTX, down), lax.ppermute(second_row, CTX, up)


def pack_keys(rows):
    lead = rows[..., :LAT].reshape(2, 128, 4, 128).transpose(0, 2, 1, 3).reshape(8, 128, 128)
    rope = jnp.concatenate([rows[0, :, LAT:KEYW], rows[1, :, LAT:KEYW]], axis=1)
    return jnp.concatenate([lead, rope[None]], axis=0)


def merge_kernel(in_ref, out_ref):
    total = in_ref[0].astype(f32)
    for t in range(1, N_XY):
        total = total + in_ref[t].astype(f32)
    total = total.astype(bf16)
    for zh in range(2):
        rope = total[8, :, zh * ROPE : (zh + 1) * ROPE]
        row = jnp.concatenate(
            [total[zh * 4 + c] for c in range(4)] + [rope, jnp.zeros_like(rope)], axis=1
        )
        for z in range(4):
            out_ref[zh * 4 + z] = row[z * PIECE : (z + 1) * PIECE]


def merge(arrived):
    return pl.pallas_call(
        merge_kernel,
        out_shape=jax.ShapeDtypeStruct((N_Z, PIECE, WIDE), bf16),
        compiler_params=pltpu.CompilerParams(vmem_limit_bytes=16 * 1024 * 1024),
        cost_estimate=pl.CostEstimate(
            flops=1_200_000, bytes_accessed=2_500_000, transcendentals=0
        ),
        name="merge",
    )(arrived)


def attention_kernel(
    where_ref,
    mine_ref,
    other_ref,
    q_hbm,
    qt_hbm,
    g_hbm,
    gt_hbm,
    ot_hbm,
    leadt_hbm,
    tailt_hbm,
    dmine_ref,
    dother_ref,
    keys,
    q_ref,
    qt_ref,
    g_ref,
    gt_ref,
    s_buf,
    dp_buf,
    m_buf,
    l_buf,
    a_buf,
    ot_buf,
    dqt_buf,
    ot_out,
    lead_out,
    dk_buf,
    dk_out,
    sems,
    out_sems,
):
    ctx = where_ref[0]
    core = where_ref[1]
    copies = [
        pltpu.make_async_copy(source, target, sems.at[n])
        for n, (source, target) in enumerate(
            [
                (mine_ref, keys.at[core]),
                (qt_hbm, qt_ref),
                (gt_hbm, gt_ref),
                (other_ref, keys.at[1 - core]),
                (q_hbm, q_ref),
                (g_hbm, g_ref),
            ]
        )
    ]
    for copy in copies:
        copy.start()
    m_buf[...] = jnp.full_like(m_buf, -jnp.inf)
    l_buf[...] = jnp.zeros_like(l_buf)
    a_buf[...] = jnp.zeros_like(a_buf)
    ot_buf[...] = jnp.zeros_like(ot_buf)
    dqt_buf[...] = jnp.zeros_like(dqt_buf)

    def clear(t, carry):
        dk_buf[0, t] = jnp.zeros((9, 64, 128), f32)
        dk_buf[1, t] = jnp.zeros((9, 64, 128), f32)
        return carry

    lax.fori_loop(0, N_XY, clear, 0)
    for copy in copies[:4]:
        copy.wait()

    group = ctx // 8
    early_steps = group + 1

    def locate(i):
        late = i >= early_steps
        j = i - early_steps
        half = jnp.logical_and(late, j >= 4).astype(jnp.int32)
        block = jnp.where(late, jnp.where(j >= 4, group + j - 4, j), i)
        return late.astype(jnp.int32), half, block

    def slab(half, block):
        xh = block // 2
        at = pl.multiple_of((block % 2) * 64, 64)

        def tile(part):
            return jnp.concatenate(
                [
                    keys[co, half * 4 + y, part, pl.ds(at, 64), :]
                    for co in range(2)
                    for y in range(4)
                ],
                axis=0,
            )

        rope = tile(8)
        rope = jnp.where(xh == 0, rope[:, :ROPE], rope[:, ROPE:])
        return jnp.concatenate([tile(xh * 4 + c) for c in range(4)] + [rope], axis=1)

    def nn(a, b):
        return jnp.dot(a, b, preferred_element_type=f32)

    def first(i, carry):
        seg, half, block = locate(i)
        k = slab(half, block)
        idx = lax.broadcasted_iota(jnp.int32, (BLOCK, 1), 0)
        owner = block * 8 + ((idx // 16) % 4) * 2 + idx // 256
        within = ((idx // 64) % 4) * 16 + idx % 16
        key_pos = jnp.where(half == 0, owner, 63 - owner) * 64 + within
        wide = SEG // 1
        row = lax.broadcasted_iota(jnp.int32, (1, wide), 1)
        q_pos = jnp.where(seg == 0, ctx, 63 - ctx) * 64 + row % 64
        for at in range(0, SEG, wide):
            part = slice(at, at + wide)
            s = nn(k, qt_ref[seg, :, part]) * (SCALE * LOG2E)
            s = jnp.where(key_pos <= q_pos, s, -jnp.inf)
            s_buf[i, :, part] = s
            dp = nn(k[:, :LAT], gt_ref[seg, :, part])
            dp_buf[i, :, part] = dp
            m_old = m_buf[seg, :, part]
            m_new = jnp.maximum(m_old, jnp.max(s, axis=0, keepdims=True))
            alpha = jnp.exp2(m_old - m_new)
            e = jnp.exp2(s - m_new)
            m_buf[seg, :, part] = m_new
            l_buf[seg, :, part] = l_buf[seg, :, part] * alpha + jnp.sum(e, axis=0, keepdims=True)
            a_buf[seg, :, part] = a_buf[seg, :, part] * alpha + jnp.sum(
                e * dp, axis=0, keepdims=True
            )
        return carry

    lax.fori_loop(0, STEPS, first, 0)
    for copy in copies[4:]:
        copy.wait()
    a_buf[...] = a_buf[...] / l_buf[...]
    m_buf[...] = m_buf[...] + jnp.log2(l_buf[...])

    def second(i, carry):
        seg, half, block = locate(i)
        k = slab(half, block)
        kt = k.T
        wide = SEG // 1
        lead = None
        for at in range(0, SEG, wide):
            part = slice(at, at + wide)
            p = jnp.exp2(s_buf[i, :, part] - m_buf[seg, :, part]).astype(bf16)
            ds = (p.astype(f32) * ((dp_buf[i, :, part] - a_buf[seg, :, part]) * SCALE)).astype(bf16)
            ot_buf[seg, :, part] += nn(kt[:LAT], p)
            dqt_buf[seg, :, part] += nn(kt, ds)
            more = nn(ds, q_ref[seg, part, :LAT]) + nn(p, g_ref[seg, part, :])
            rest = nn(ds, q_ref[seg, part, LAT:])
            lead = more if lead is None else lead + more
            tail = rest if at == 0 else tail + rest
        x4 = (block // 2 * 2 + half) * 4
        zh = block % 2
        lane = lax.broadcasted_iota(jnp.int32, (1, 128), 1)
        tail = jnp.where(lane // ROPE == zh, jnp.concatenate([tail, tail], axis=1), 0.0)
        for co in range(2):
            for y in range(4):
                j = (co * 4 + y) * 64
                for c in range(4):
                    dk_buf[co, x4 + y, zh * 4 + c] += lead[j : j + 64, c * 128 : c * 128 + 128]
                dk_buf[co, x4 + y, 8] += tail[j : j + 64]
        return carry

    lax.fori_loop(0, STEPS, second, 0)

    sends = []

    def send(source, target):
        copy = pltpu.make_async_copy(source, target, out_sems.at[len(sends)])
        copy.start()
        sends.append(copy)

    send(dqt_buf.at[:, pl.ds(LAT, ROPE)], tailt_hbm)
    for t in range(0, N_XY, 2):
        dk_out[0, t : t + 2] = dk_buf[1 - core, t : t + 2].astype(bf16)
        send(dk_out.at[0, pl.ds(t, 2)], dother_ref.at[pl.ds(t, 2)])
    for t in range(0, N_XY, 2):
        dk_out[1, t : t + 2] = dk_buf[core, t : t + 2].astype(bf16)
        send(dk_out.at[1, pl.ds(t, 2)], dmine_ref.at[pl.ds(t, 2)])
    for seg in range(2):
        ot_out[seg] = ot_buf[seg].astype(bf16)
        send(ot_out.at[seg], ot_hbm.at[seg])
        lead_out[seg] = dqt_buf[seg, :LAT].astype(bf16)
        send(lead_out.at[seg], leadt_hbm.at[seg])
    for copy in sends:
        copy.wait()


def attention(where, mine, other, q, qt, g, gt):
    hbm = pl.BlockSpec(memory_space=pl.ANY)
    half_keys = (N_TP, 9, 128, 128)
    half_grads = (N_XY, 9, 64, 128)
    return pl.pallas_call(
        attention_kernel,
        in_specs=[pl.BlockSpec(memory_space=pltpu.SMEM)] + [hbm] * 6,
        out_specs=[hbm] * 5,
        out_shape=[
            jax.ShapeDtypeStruct((2, LAT, SEG), bf16),
            jax.ShapeDtypeStruct((2, LAT, SEG), bf16),
            jax.ShapeDtypeStruct((2, ROPE, SEG), f32),
            jax.ShapeDtypeStruct(half_grads, bf16),
            jax.ShapeDtypeStruct(half_grads, bf16),
        ],
        scratch_shapes=[
            pltpu.VMEM((2,) + half_keys, bf16),
            pltpu.VMEM((2, SEG, KEYW), bf16),
            pltpu.VMEM((2, KEYW, SEG), bf16),
            pltpu.VMEM((2, SEG, LAT), bf16),
            pltpu.VMEM((2, LAT, SEG), bf16),
            pltpu.VMEM((STEPS, BLOCK, SEG), f32),
            pltpu.VMEM((STEPS, BLOCK, SEG), f32),
            pltpu.VMEM((2, 1, SEG), f32),
            pltpu.VMEM((2, 1, SEG), f32),
            pltpu.VMEM((2, 1, SEG), f32),
            pltpu.VMEM((2, LAT, SEG), f32),
            pltpu.VMEM((2, KEYW, SEG), f32),
            pltpu.VMEM((2, LAT, SEG), bf16),
            pltpu.VMEM((2, LAT, SEG), bf16),
            pltpu.VMEM((2,) + half_grads, f32),
            pltpu.VMEM((2,) + half_grads, bf16),
            pltpu.SemaphoreType.DMA((6,)),
            pltpu.SemaphoreType.DMA((21,)),
        ],
        compiler_params=pltpu.CompilerParams(vmem_limit_bytes=60 * 1024 * 1024),
        cost_estimate=pl.CostEstimate(
            flops=14_000_000_000, bytes_accessed=20_000_000, transcendentals=4_000_000
        ),
        name="attention",
    )(where, mine, other, q, qt, g, gt)


def on_device(
    hidden,
    embed,
    gain_hidden,
    gain_embed,
    proj_hidden,
    proj_embed,
    gain_latent,
    key_up,
    value_up,
    queries,
    grad_out,
):
    ctx = lax.axis_index(CTX)
    core = lax.axis_index("co")
    tp = lax.axis_index(TP)
    last = ctx == N_CTX - 1

    after, before = edge_exchange(embed[0:1], embed[HALF : HALF + 1])
    after_early = jnp.where(last, embed[HALF : HALF + 1], after)
    next_embed = jnp.concatenate(
        [embed[1:HALF], after_early, embed[HALF + 1 :], before], axis=0
    )
    hidden_wide = hidden.astype(f32)
    next_wide = next_embed.astype(f32)
    part_hidden = jnp.dot(
        (hidden_wide * gain_hidden).astype(bf16), proj_hidden, preferred_element_type=f32
    )
    part_next = jnp.dot(
        (next_wide * gain_embed).astype(bf16), proj_embed, preferred_element_type=f32
    )
    spread = (ROWS, WIDE - KEYW)
    parts = jnp.concatenate(
        [
            part_hidden,
            jnp.broadcast_to(jnp.sum(hidden_wide * hidden_wide, axis=1, keepdims=True), spread),
            part_next,
            jnp.broadcast_to(jnp.sum(next_wide * next_wide, axis=1, keepdims=True), spread),
        ],
        axis=1,
    ).reshape(N_TP, PIECE, 2 * WIDE)
    parts = lax.all_to_all(parts, TP, split_axis=0, concat_axis=0, tiled=True)

    parts, queries, grad_out = lax.optimization_barrier((parts, queries, grad_out))
    parts = jnp.sum(parts, axis=0)
    part_hidden, part_next = parts[:, :KEYW], parts[:, WIDE : WIDE + KEYW]
    inv_hidden = lax.rsqrt(parts[:, KEYW : KEYW + 1] / D + EPSILON)
    inv_next = lax.rsqrt(parts[:, WIDE + KEYW : WIDE + KEYW + 1] / D + EPSILON)
    latent = inv_hidden * part_hidden + inv_next * part_next
    leading = latent[:, :LAT]
    inv_latent = lax.rsqrt(jnp.mean(leading * leading, axis=1, keepdims=True) + EPSILON)
    piece_cos, piece_sin = rotation(row_positions(ctx, tp * PIECE + jnp.arange(PIECE)))
    key_piece = jnp.concatenate(
        [
            (leading * inv_latent * gain_latent).astype(bf16),
            rotate_pairs(latent[:, LAT:], piece_cos, piece_sin).astype(bf16),
            jnp.zeros((PIECE, WIDE - KEYW), bf16),
        ],
        axis=1,
    )
    same = pack_keys(gather_copies(key_piece, XZ, 16).reshape(2, 128, WIDE))
    mine = gather_copies(same, TP, N_TP)

    cos_table, sin_table = rotation(row_positions(ctx, jnp.arange(ROWS)))
    cos_table = cos_table.reshape(2, 1, HALF, ROPE // 2)
    sin_table = sin_table.reshape(2, 1, HALF, ROPE // 2)
    key_up_heads = key_up.reshape(LAT, HEADS, NOPE)
    value_up_heads = value_up.reshape(LAT, HEADS, VDIM)
    query_heads = queries.reshape(2, HALF, HEADS, NOPE + ROPE).transpose(0, 2, 1, 3)
    query_rot = rotate_pairs(query_heads[..., NOPE:].astype(f32), cos_table, sin_table)
    query_latent = jnp.einsum(
        "ghsn,lhn->ghsl", query_heads[..., :NOPE], key_up_heads, preferred_element_type=f32
    )
    q = jnp.concatenate([query_latent.astype(bf16), query_rot.astype(bf16)], axis=3)
    q = q.reshape(2, SEG, KEYW)
    g = jnp.einsum(
        "gshv,lhv->ghsl",
        grad_out.reshape(2, HALF, HEADS, VDIM),
        value_up_heads,
        preferred_element_type=f32,
    )
    g = g.astype(bf16).reshape(2, SEG, LAT)
    qt, gt = q.swapaxes(1, 2), g.swapaxes(1, 2)
    mine, q, qt, g, gt = lax.optimization_barrier((mine, q, qt, g, gt))
    other = lax.ppermute(mine, "co", [(0, 1), (1, 0)])

    where = jnp.stack([ctx, core]).astype(jnp.int32)
    ot, leadt, tailt, dmine, dother = attention(
        where, mine, other, q, qt, g, gt
    )

    received = lax.ppermute(dother, "co", [(0, 1), (1, 0)])
    dkey = (dmine.astype(f32) + received.astype(f32)).astype(bf16)
    dkey = lax.all_to_all(dkey, XY, split_axis=0, concat_axis=0, tiled=True)

    attended = jnp.einsum(
        "glhs,lhv->gshv",
        ot.reshape(2, LAT, HEADS, HALF),
        value_up_heads,
        preferred_element_type=f32,
    )
    attended = attended.astype(bf16).reshape(ROWS, HEADS * VDIM)
    grad_nope = jnp.einsum(
        "glhs,lhn->ghsn",
        leadt.reshape(2, LAT, HEADS, HALF),
        key_up_heads,
        preferred_element_type=f32,
    )
    grad_rope = unrotate(
        tailt.reshape(2, ROPE, HEADS, HALF).transpose(0, 2, 3, 1), cos_table, sin_table
    )
    grad_queries = jnp.concatenate([grad_nope, grad_rope], axis=3).astype(bf16)
    grad_queries = grad_queries.transpose(0, 2, 1, 3).reshape(ROWS, HEADS * (NOPE + ROPE))
    dkey, attended, grad_queries = lax.optimization_barrier((dkey, attended, grad_queries))

    dkey = lax.all_to_all(merge(dkey), "z", split_axis=0, concat_axis=0, tiled=True)
    dkey = jnp.sum(dkey.astype(f32), axis=0)[:, :KEYW]

    gained = gain_latent * dkey[:, :LAT]
    dlatent = jnp.concatenate(
        [
            inv_latent * gained
            - inv_latent**3 * leading * jnp.sum(gained * leading, axis=1, keepdims=True) / LAT,
            unrotate(dkey[:, LAT:], piece_cos, piece_sin),
        ],
        axis=1,
    )
    coef_hidden = jnp.sum(dlatent * part_hidden, axis=1, keepdims=True) * inv_hidden**3 / D
    coef_next = jnp.sum(dlatent * part_next, axis=1, keepdims=True) * inv_next**3 / D

    def in_two(c):
        high = lax.reduce_precision(c, 8, 7)
        low = c - high
        width = (PIECE, (WIDE - KEYW) // 2)
        return [jnp.broadcast_to(h.astype(bf16), width) for h in (high, low)]

    packed_hidden = jnp.concatenate(
        [(inv_hidden * dlatent).astype(bf16)] + in_two(coef_hidden), axis=1
    )
    packed_next = jnp.concatenate(
        [(inv_next * dlatent).astype(bf16)] + in_two(coef_next), axis=1
    )
    before = lax.ppermute(packed_next[-1:], ALL, list(zip(ORDER[:-1], ORDER[1:])))
    packed = jnp.concatenate(
        [packed_hidden, jnp.concatenate([before, packed_next[:-1]], axis=0)], axis=1
    )
    packed = gather_copies(packed, TP, N_TP).reshape(ROWS, 2 * WIDE)

    def whole(block):
        high = block[:, KEYW : KEYW + 1].astype(f32)
        return block[:, :KEYW], high + block[:, WIDE - 1 :].astype(f32)

    dpart_hidden, coef_hidden = whole(packed[:, :WIDE])
    grad_hidden = (
        gain_hidden
        * jnp.einsum("rc,dc->rd", dpart_hidden, proj_hidden, preferred_element_type=f32)
        - coef_hidden * hidden_wide
    ).astype(bf16)

    dpart_next, coef_next = whole(packed[:, WIDE:])
    grad_embed = (
        gain_embed
        * jnp.einsum("rc,dc->rd", dpart_next, proj_embed, preferred_element_type=f32)
        - coef_next * embed.astype(f32)
    ).astype(bf16)
    return (attended, grad_queries, grad_hidden, grad_embed)


def solution(mesh):
    axes = ("xh", "z", "co", "xl", "y")
    fine = Mesh(mesh.devices.reshape(2, 8, 2, 2, 4), axes)
    both = P(CTX, TP)
    placed = (
        both,
        both,
        P(TP),
        P(TP),
        P(TP, None),
        P(TP, None),
        P(),
        P(None, TP),
        P(None, TP),
        both,
        both,
    )
    return jax.shard_map(
        on_device,
        mesh=fine,
        in_specs=placed,
        out_specs=(both, both, both, both),
        check_vma=False,
    )
```

```python
import functools

import jax
import jax.numpy as jnp
from jax import lax
from jax.experimental import pallas as pl
from jax.experimental.pallas import tpu as pltpu
from jax.sharding import Mesh, PartitionSpec as P

D = 7168
LAT = 512
ROPE = 64
NOPE = 128
VDIM = 128
KEYW = LAT + ROPE
WIDE = 640

EPSILON = 1e-06
ROTARY_BASE = 10000.0
SCALE = (NOPE + ROPE) ** (-0.5)
LOG2E = 1.4426950408889634

CTX = ("xh", "z", "co")
TP = ("xl", "y")
XZ = ("xh", "z")
XY = ("xh", "xl", "y")
N_CTX = 32
N_TP = 8
N_Z = 8
N_XY = 16
HEADS = 8
HALF = 64
ROWS = 128
PIECE = ROWS // N_TP
SEG = HALF * HEADS
BLOCK = 512
STEPS = 9

ALL = CTX + TP
ORDER = [c * N_TP + t for c in range(N_CTX) for t in range(N_TP // 2)] + [
    c * N_TP + t for c in reversed(range(N_CTX)) for t in range(N_TP // 2, N_TP)
]

bf16 = jnp.bfloat16
f32 = jnp.float32


def rotation(positions):
    pair_count = ROPE // 2
    frequency = ROTARY_BASE ** (-jnp.arange(pair_count, dtype=f32) / pair_count)
    angles = positions.astype(f32)[:, None] * frequency[None, :]
    return (jnp.cos(angles), jnp.sin(angles))


def rotate_pairs(values, cos_table, sin_table):
    a, b = jnp.split(values, 2, axis=-1)
    return jnp.concatenate(
        [a * cos_table - b * sin_table, a * sin_table + b * cos_table], axis=-1
    )


def unrotate(values, cos_table, sin_table):
    a, b = jnp.split(values, 2, axis=-1)
    return jnp.concatenate(
        [a * cos_table + b * sin_table, b * cos_table - a * sin_table], axis=-1
    )


def row_positions(ctx, rows):
    return jnp.where(rows < HALF, ctx * HALF + rows, (63 - ctx) * HALF + rows - HALF)


def gather_copies(x, axes, n):
    copies = jnp.broadcast_to(x[None], (n, *x.shape))
    return lax.all_to_all(copies, axes, split_axis=0, concat_axis=0, tiled=True)


def edge_exchange(first_row, second_row):
    down = [(i + 1, i) for i in range(N_CTX - 1)]
    up = [(i, i + 1) for i in range(N_CTX - 1)]
    return lax.ppermute(first_row, CTX, down), lax.ppermute(second_row, CTX, up)


def project_kernel(
    where_ref, hidden_ref, embed_ref, after_ref, before_ref, gh_ref, ge_ref, ph_ref, pe_ref, out_ref
):
    def put(at, values, gain, weights):
        squares = jnp.sum(values * values, axis=1, keepdims=True)
        scaled = (values * gain).astype(bf16)
        out_ref[:, at : at + KEYW] = lax.dot_general(
            scaled, weights, (((1,), (1,)), ((), ())), preferred_element_type=f32
        )
        out_ref[:, at + KEYW : at + WIDE] = jnp.broadcast_to(squares, (ROWS, WIDE - KEYW))

    put(0, hidden_ref[...].astype(f32), gh_ref[...], ph_ref[...])
    own = embed_ref[...].astype(f32)
    row = lax.broadcasted_iota(jnp.int32, (ROWS, 1), 0)
    after = jnp.where(
        where_ref[0] == N_CTX - 1, own[HALF : HALF + 1], after_ref[...].astype(f32)
    )
    following = jnp.where(row == HALF - 1, after, pltpu.roll(own, ROWS - 1, 0))
    following = jnp.where(row == ROWS - 1, before_ref[...].astype(f32), following)
    put(WIDE, following, ge_ref[...], pe_ref[...])


def project(where, *operands):
    vmem = pl.BlockSpec(memory_space=pltpu.VMEM)
    return pl.pallas_call(
        project_kernel,
        in_specs=[pl.BlockSpec(memory_space=pltpu.SMEM)] + [vmem] * 8,
        out_specs=vmem,
        out_shape=jax.ShapeDtypeStruct((ROWS, 2 * WIDE), f32),
        compiler_params=pltpu.CompilerParams(vmem_limit_bytes=60 * 1024 * 1024),
        cost_estimate=pl.CostEstimate(
            flops=270_000_000, bytes_accessed=3_200_000, transcendentals=0
        ),
        name="project",
    )(where, *operands)


def pack_keys(rows):
    lead = rows[..., :LAT].reshape(2, 128, 4, 128).transpose(0, 2, 1, 3).reshape(8, 128, 128)
    rope = jnp.concatenate([rows[0, :, LAT:KEYW], rows[1, :, LAT:KEYW]], axis=1)
    return jnp.concatenate([lead, rope[None]], axis=0)


def merge_kernel(in_ref, out_ref):
    total = in_ref[0].astype(f32)
    for t in range(1, N_XY):
        total = total + in_ref[t].astype(f32)
    total = total.astype(bf16)
    for zh in range(2):
        rope = total[8, :, zh * ROPE : (zh + 1) * ROPE]
        row = jnp.concatenate(
            [total[zh * 4 + c] for c in range(4)] + [rope, jnp.zeros_like(rope)], axis=1
        )
        for z in range(4):
            out_ref[zh * 4 + z] = row[z * PIECE : (z + 1) * PIECE]


def merge(arrived):
    return pl.pallas_call(
        merge_kernel,
        out_shape=jax.ShapeDtypeStruct((N_Z, PIECE, WIDE), bf16),
        compiler_params=pltpu.CompilerParams(vmem_limit_bytes=16 * 1024 * 1024),
        cost_estimate=pl.CostEstimate(
            flops=1_200_000, bytes_accessed=2_500_000, transcendentals=0
        ),
        name="merge",
    )(arrived)


def attention_kernel(
    where_ref,
    mine_ref,
    other_ref,
    q_hbm,
    qt_hbm,
    g_hbm,
    gt_hbm,
    ot_hbm,
    leadt_hbm,
    tailt_hbm,
    dmine_ref,
    dother_ref,
    keys,
    q_ref,
    qt_ref,
    g_ref,
    gt_ref,
    s_buf,
    dp_buf,
    m_buf,
    l_buf,
    a_buf,
    ot_buf,
    dqt_buf,
    ot_out,
    lead_out,
    tail_out,
    dk_buf,
    dk_out,
    sems,
    out_sems,
):
    ctx = where_ref[0]
    core = where_ref[1]
    copies = [
        pltpu.make_async_copy(source, target, sems.at[n])
        for n, (source, target) in enumerate(
            [
                (mine_ref.at[pl.ds(0, 4)], keys.at[core, pl.ds(0, 4)]),
                (other_ref.at[pl.ds(0, 4)], keys.at[1 - core, pl.ds(0, 4)]),
                (qt_hbm, qt_ref),
                (gt_hbm, gt_ref),
                (mine_ref.at[pl.ds(4, 4)], keys.at[core, pl.ds(4, 4)]),
                (other_ref.at[pl.ds(4, 4)], keys.at[1 - core, pl.ds(4, 4)]),
                (q_hbm, q_ref),
                (g_hbm, g_ref),
            ]
        )
    ]
    for copy in copies:
        copy.start()
    m_buf[...] = jnp.full_like(m_buf, -jnp.inf)
    l_buf[...] = jnp.zeros_like(l_buf)
    a_buf[...] = jnp.zeros_like(a_buf)
    ot_buf[...] = jnp.zeros_like(ot_buf)
    dqt_buf[...] = jnp.zeros_like(dqt_buf)

    def clear(t, carry):
        dk_buf[0, t] = jnp.zeros((9, 64, 128), f32)
        dk_buf[1, t] = jnp.zeros((9, 64, 128), f32)
        return carry

    lax.fori_loop(0, N_XY, clear, 0)
    for copy in copies[:4]:
        copy.wait()

    group = ctx // 8
    early_steps = group + 1

    def locate(i):
        late = i >= early_steps
        j = i - early_steps
        half = jnp.logical_and(late, j >= 4).astype(jnp.int32)
        block = jnp.where(late, jnp.where(j >= 4, group + j - 4, j), i)
        return late.astype(jnp.int32), half, block

    def slab(half, block):
        xh = block // 2
        at = pl.multiple_of((block % 2) * 64, 64)

        def tile(part):
            return jnp.concatenate(
                [
                    keys[co, half * 4 + y, part, pl.ds(at, 64), :]
                    for co in range(2)
                    for y in range(4)
                ],
                axis=0,
            )

        rope = tile(8)
        rope = jnp.where(xh == 0, rope[:, :ROPE], rope[:, ROPE:])
        return jnp.concatenate([tile(xh * 4 + c) for c in range(4)] + [rope], axis=1)

    def nn(a, b):
        return jnp.dot(a, b, preferred_element_type=f32)

    def first(i, carry):
        @pl.when(i == early_steps + 4)
        def _():
            for copy in copies[4:6]:
                copy.wait()

        seg, half, block = locate(i)
        k = slab(half, block)
        idx = lax.broadcasted_iota(jnp.int32, (BLOCK, 1), 0)
        owner = block * 8 + ((idx // 16) % 4) * 2 + idx // 256
        within = ((idx // 64) % 4) * 16 + idx % 16
        key_pos = jnp.where(half == 0, owner, 63 - owner) * 64 + within
        wide = SEG // 1
        row = lax.broadcasted_iota(jnp.int32, (1, wide), 1)
        q_pos = jnp.where(seg == 0, ctx, 63 - ctx) * 64 + row % 64
        for at in range(0, SEG, wide):
            part = slice(at, at + wide)
            s = nn(k, qt_ref[seg, :, part]) * (SCALE * LOG2E)
            s = jnp.where(key_pos <= q_pos, s, -jnp.inf)
            s_buf[i, :, part] = s
            dp = nn(k[:, :LAT], gt_ref[seg, :, part])
            dp_buf[i, :, part] = dp
            m_old = m_buf[seg, :, part]
            m_new = jnp.maximum(m_old, jnp.max(s, axis=0, keepdims=True))
            alpha = jnp.exp2(m_old - m_new)
            e = jnp.exp2(s - m_new)
            m_buf[seg, :, part] = m_new
            l_buf[seg, :, part] = l_buf[seg, :, part] * alpha + jnp.sum(e, axis=0, keepdims=True)
            a_buf[seg, :, part] = a_buf[seg, :, part] * alpha + jnp.sum(
                e * dp, axis=0, keepdims=True
            )
        return carry

    lax.fori_loop(0, STEPS, first, 0)
    for copy in copies[6:]:
        copy.wait()
    a_buf[...] = a_buf[...] / l_buf[...]
    m_buf[...] = m_buf[...] + jnp.log2(l_buf[...])

    sends = []

    def send(source, target):
        sends.append(pltpu.make_async_copy(source, target, out_sems.at[len(sends)]))

    for xl in range(2):
        for core_first, target in ((0, dother_ref), (1, dmine_ref)):
            for xh in range(2):
                four = pl.ds((xh * 2 + xl) * 4, 4)
                send(dk_out.at[core_first, four], target.at[four])
    for seg in range(2):
        send(ot_out.at[seg], ot_hbm.at[seg])
        send(lead_out.at[seg], leadt_hbm.at[seg])
        send(tail_out.at[seg], tailt_hbm.at[seg])

    def put_keys(xl):
        for slot, source in ((0, 1 - core), (1, core)):
            for xh in range(2):
                at = (xh * 2 + xl) * 4
                dk_out[slot, at : at + 4] = dk_buf[source, at : at + 4].astype(bf16)
                sends[xl * 4 + slot * 2 + xh].start()

    def put_rows(seg):
        ot_out[seg] = ot_buf[seg].astype(bf16)
        lead_out[seg] = dqt_buf[seg, :LAT].astype(bf16)
        tail_out[seg] = dqt_buf[seg, LAT:]
        for copy in sends[8 + seg * 3 : 11 + seg * 3]:
            copy.start()

    def second(i, carry):
        @pl.when(i == early_steps)
        def _():
            put_rows(0)

        @pl.when(i == early_steps + 4)
        def _():
            put_keys(0)

        seg, half, block = locate(i)
        k = slab(half, block)
        kt = k.T
        wide = SEG // 1
        lead = None
        for at in range(0, SEG, wide):
            part = slice(at, at + wide)
            p = jnp.exp2(s_buf[i, :, part] - m_buf[seg, :, part]).astype(bf16)
            ds = (p.astype(f32) * ((dp_buf[i, :, part] - a_buf[seg, :, part]) * SCALE)).astype(bf16)
            ot_buf[seg, :, part] += nn(kt[:LAT], p)
            dqt_buf[seg, :, part] += nn(kt, ds)
            more = nn(ds, q_ref[seg, part, :LAT]) + nn(p, g_ref[seg, part, :])
            rest = nn(ds, q_ref[seg, part, LAT:])
            lead = more if lead is None else lead + more
            tail = rest if at == 0 else tail + rest
        x4 = (block // 2 * 2 + half) * 4
        zh = block % 2
        lane = lax.broadcasted_iota(jnp.int32, (1, 128), 1)
        tail = jnp.where(lane // ROPE == zh, jnp.concatenate([tail, tail], axis=1), 0.0)
        for co in range(2):
            for y in range(4):
                j = (co * 4 + y) * 64
                for c in range(4):
                    dk_buf[co, x4 + y, zh * 4 + c] += lead[j : j + 64, c * 128 : c * 128 + 128]
                dk_buf[co, x4 + y, 8] += tail[j : j + 64]
        return carry

    lax.fori_loop(0, STEPS, second, 0)

    put_keys(1)
    put_rows(1)
    for copy in sends:
        copy.wait()


def attention(where, mine, other, q, qt, g, gt):
    hbm = pl.BlockSpec(memory_space=pl.ANY)
    half_keys = (N_TP, 9, 128, 128)
    half_grads = (N_XY, 9, 64, 128)
    return pl.pallas_call(
        attention_kernel,
        in_specs=[pl.BlockSpec(memory_space=pltpu.SMEM)] + [hbm] * 6,
        out_specs=[hbm] * 5,
        out_shape=[
            jax.ShapeDtypeStruct((2, LAT, SEG), bf16),
            jax.ShapeDtypeStruct((2, LAT, SEG), bf16),
            jax.ShapeDtypeStruct((2, ROPE, SEG), f32),
            jax.ShapeDtypeStruct(half_grads, bf16),
            jax.ShapeDtypeStruct(half_grads, bf16),
        ],
        scratch_shapes=[
            pltpu.VMEM((2,) + half_keys, bf16),
            pltpu.VMEM((2, SEG, KEYW), bf16),
            pltpu.VMEM((2, KEYW, SEG), bf16),
            pltpu.VMEM((2, SEG, LAT), bf16),
            pltpu.VMEM((2, LAT, SEG), bf16),
            pltpu.VMEM((STEPS, BLOCK, SEG), f32),
            pltpu.VMEM((STEPS, BLOCK, SEG), f32),
            pltpu.VMEM((2, 1, SEG), f32),
            pltpu.VMEM((2, 1, SEG), f32),
            pltpu.VMEM((2, 1, SEG), f32),
            pltpu.VMEM((2, LAT, SEG), f32),
            pltpu.VMEM((2, KEYW, SEG), f32),
            pltpu.VMEM((2, LAT, SEG), bf16),
            pltpu.VMEM((2, LAT, SEG), bf16),
            pltpu.VMEM((2, ROPE, SEG), f32),
            pltpu.VMEM((2,) + half_grads, f32),
            pltpu.VMEM((2,) + half_grads, bf16),
            pltpu.SemaphoreType.DMA((8,)),
            pltpu.SemaphoreType.DMA((14,)),
        ],
        compiler_params=pltpu.CompilerParams(vmem_limit_bytes=60 * 1024 * 1024),
        cost_estimate=pl.CostEstimate(
            flops=14_000_000_000, bytes_accessed=20_000_000, transcendentals=4_000_000
        ),
        name="attention",
    )(where, mine, other, q, qt, g, gt)


def on_device(
    hidden,
    embed,
    gain_hidden,
    gain_embed,
    proj_hidden,
    proj_embed,
    gain_latent,
    key_up,
    value_up,
    queries,
    grad_out,
):
    ctx = lax.axis_index(CTX)
    core = lax.axis_index("co")
    tp = lax.axis_index(TP)

    after, before = edge_exchange(embed[0:1], embed[HALF : HALF + 1])
    where = jnp.stack([ctx, core]).astype(jnp.int32)
    parts = project(
        where,
        hidden,
        embed,
        after,
        before,
        gain_hidden[None],
        gain_embed[None],
        proj_hidden.T,
        proj_embed.T,
    ).reshape(N_TP, PIECE, 2 * WIDE)
    parts = lax.all_to_all(parts, TP, split_axis=0, concat_axis=0, tiled=True)

    parts, queries, grad_out = lax.optimization_barrier((parts, queries, grad_out))
    parts = jnp.sum(parts, axis=0)
    part_hidden, part_next = parts[:, :KEYW], parts[:, WIDE : WIDE + KEYW]
    inv_hidden = lax.rsqrt(parts[:, KEYW : KEYW + 1] / D + EPSILON)
    inv_next = lax.rsqrt(parts[:, WIDE + KEYW : WIDE + KEYW + 1] / D + EPSILON)
    latent = inv_hidden * part_hidden + inv_next * part_next
    leading = latent[:, :LAT]
    inv_latent = lax.rsqrt(jnp.mean(leading * leading, axis=1, keepdims=True) + EPSILON)
    piece_cos, piece_sin = rotation(row_positions(ctx, tp * PIECE + jnp.arange(PIECE)))
    key_piece = jnp.concatenate(
        [
            (leading * inv_latent * gain_latent).astype(bf16),
            rotate_pairs(latent[:, LAT:], piece_cos, piece_sin).astype(bf16),
            jnp.zeros((PIECE, WIDE - KEYW), bf16),
        ],
        axis=1,
    )
    same = pack_keys(gather_copies(key_piece, XZ, 16).reshape(2, 128, WIDE))
    mine = gather_copies(same, TP, N_TP)

    cos_table, sin_table = rotation(row_positions(ctx, jnp.arange(ROWS)))
    cos_table = cos_table.reshape(2, 1, HALF, ROPE // 2)
    sin_table = sin_table.reshape(2, 1, HALF, ROPE // 2)
    key_up_heads = key_up.reshape(LAT, HEADS, NOPE)
    value_up_heads = value_up.reshape(LAT, HEADS, VDIM)
    query_heads = queries.reshape(2, HALF, HEADS, NOPE + ROPE).transpose(0, 2, 1, 3)
    query_rot = rotate_pairs(query_heads[..., NOPE:].astype(f32), cos_table, sin_table)
    query_latent = jnp.einsum(
        "ghsn,lhn->ghsl", query_heads[..., :NOPE], key_up_heads, preferred_element_type=f32
    )
    q = jnp.concatenate([query_latent.astype(bf16), query_rot.astype(bf16)], axis=3)
    q = q.reshape(2, SEG, KEYW)
    g = jnp.einsum(
        "gshv,lhv->ghsl",
        grad_out.reshape(2, HALF, HEADS, VDIM),
        value_up_heads,
        preferred_element_type=f32,
    )
    g = g.astype(bf16).reshape(2, SEG, LAT)
    qt, gt = q.swapaxes(1, 2), g.swapaxes(1, 2)
    mine, q, qt, g, gt = lax.optimization_barrier((mine, q, qt, g, gt))
    other = lax.ppermute(mine, "co", [(0, 1), (1, 0)])

    ot, leadt, tailt, dmine, dother = attention(
        where, mine, other, q, qt, g, gt
    )

    received = lax.ppermute(dother, "co", [(0, 1), (1, 0)])
    dkey = (dmine.astype(f32) + received.astype(f32)).astype(bf16)
    dkey = lax.all_to_all(dkey, XY, split_axis=0, concat_axis=0, tiled=True)

    attended = jnp.einsum(
        "glhs,lhv->gshv",
        ot.reshape(2, LAT, HEADS, HALF),
        value_up_heads,
        preferred_element_type=f32,
    )
    attended = attended.astype(bf16).reshape(ROWS, HEADS * VDIM)
    grad_nope = jnp.einsum(
        "glhs,lhn->ghsn",
        leadt.reshape(2, LAT, HEADS, HALF),
        key_up_heads,
        preferred_element_type=f32,
    )
    grad_rope = unrotate(
        tailt.reshape(2, ROPE, HEADS, HALF).transpose(0, 2, 3, 1), cos_table, sin_table
    )
    grad_queries = jnp.concatenate([grad_nope, grad_rope], axis=3).astype(bf16)
    grad_queries = grad_queries.transpose(0, 2, 1, 3).reshape(ROWS, HEADS * (NOPE + ROPE))
    dkey, attended, grad_queries = lax.optimization_barrier((dkey, attended, grad_queries))

    dkey = lax.all_to_all(merge(dkey), "z", split_axis=0, concat_axis=0, tiled=True)
    dkey = jnp.sum(dkey.astype(f32), axis=0)[:, :KEYW]

    gained = gain_latent * dkey[:, :LAT]
    dlatent = jnp.concatenate(
        [
            inv_latent * gained
            - inv_latent**3 * leading * jnp.sum(gained * leading, axis=1, keepdims=True) / LAT,
            unrotate(dkey[:, LAT:], piece_cos, piece_sin),
        ],
        axis=1,
    )
    coef_hidden = jnp.sum(dlatent * part_hidden, axis=1, keepdims=True) * inv_hidden**3 / D
    coef_next = jnp.sum(dlatent * part_next, axis=1, keepdims=True) * inv_next**3 / D

    def in_two(c):
        high = lax.reduce_precision(c, 8, 7)
        low = c - high
        width = (PIECE, (WIDE - KEYW) // 2)
        return [jnp.broadcast_to(h.astype(bf16), width) for h in (high, low)]

    packed_hidden = jnp.concatenate(
        [(inv_hidden * dlatent).astype(bf16)] + in_two(coef_hidden), axis=1
    )
    packed_next = jnp.concatenate(
        [(inv_next * dlatent).astype(bf16)] + in_two(coef_next), axis=1
    )
    before = lax.ppermute(packed_next[-1:], ALL, list(zip(ORDER[:-1], ORDER[1:])))
    packed = jnp.concatenate(
        [packed_hidden, jnp.concatenate([before, packed_next[:-1]], axis=0)], axis=1
    )
    packed = gather_copies(packed, TP, N_TP).reshape(ROWS, 2 * WIDE)

    def whole(block):
        high = block[:, KEYW : KEYW + 1].astype(f32)
        return block[:, :KEYW], high + block[:, WIDE - 1 :].astype(f32)

    dpart_hidden, coef_hidden = whole(packed[:, :WIDE])
    grad_hidden = (
        gain_hidden
        * jnp.einsum("rc,dc->rd", dpart_hidden, proj_hidden, preferred_element_type=f32)
        - coef_hidden * hidden.astype(f32)
    ).astype(bf16)

    dpart_next, coef_next = whole(packed[:, WIDE:])
    grad_embed = (
        gain_embed
        * jnp.einsum("rc,dc->rd", dpart_next, proj_embed, preferred_element_type=f32)
        - coef_next * embed.astype(f32)
    ).astype(bf16)
    return (attended, grad_queries, grad_hidden, grad_embed)


def solution(mesh):
    axes = ("xh", "z", "co", "xl", "y")
    fine = Mesh(mesh.devices.reshape(2, 8, 2, 2, 4), axes)
    both = P(CTX, TP)
    placed = (
        both,
        both,
        P(TP),
        P(TP),
        P(TP, None),
        P(TP, None),
        P(),
        P(None, TP),
        P(None, TP),
        both,
        both,
    )
    return jax.shard_map(
        on_device,
        mesh=fine,
        in_specs=placed,
        out_specs=(both, both, both, both),
        check_vma=False,
    )
```
